512 devices in a mesh: vis: 64 (over z, y_lo, core), facet: 8 (over x, y_hi).
Axes of the slice: x: 4, y: 4 (y_hi: 2, y_lo: 2; y = y_hi * 2 + y_lo), z: 16, core: 2. Of those that a mesh axis runs over, the one named last changes fastest.
Arguments:
- image: float32 [16384, 16384], P('vis', 'facet'), may hold values from 0 to 2
- observed: float32 [2, 1048576], P(None, ('vis', 'facet')), may hold values from -6 to 6
- weights: float32 [1048576], P(('vis', 'facet')), may hold values from 0.25 to 4
- row_cell: int32 [1048576], P(('vis', 'facet')), may hold values from 0 to 8
- col_cell: int32 [1048576], P(('vis', 'facet')), may hold values from 0 to 16376, as said below
- row_offset: int32 [1048576], P(('vis', 'facet')), may hold values from 0 to 15
- col_offset: int32 [1048576], P(('vis', 'facet')), may hold values from 0 to 15
- kernel: float32 [16, 8], replicated, may hold values from 0.1 to 1
- thresholds: float32 [2], replicated, may hold values from 0.02 to 0.4
Outputs:
- updated: float32 [16384, 16384], P('vis', 'facet')
The draws below stay inside these ranges and needn't reach their ends.
Inputs may be any that keep to these rules, and one draw needn't show every extreme that they name: Visibilities arrive bucketed by uv column tile: on the device at facet index f, every col_cell lies in [f * 2048, (f + 1) * 2048), so a kernel reaches at most 7 columns into the next tile.
All inputs are finite; a program needn't handle non-finite values.
Results may differ from the reference program's by a relative error of at most 0.0003.
Values sent between devices are 32-bit elements; how exact they have to be, the bound alone decides.
A program may use at most 64 MiB of HBM per device.

```python
import math
import jax
import jax.numpy as jnp
from jax import lax

NPIX = 16384
ROWS = 16
VIS_DEV = 2048
KW = 8
OVERSAMPLE = 16
LEVELS = 2
VISIBILITIES = 1048576
N_FACET = 8


def draw_col_cell(key, part):
    key = jax.random.fold_in(key, 11)
    facet_cols = NPIX // N_FACET
    position = jnp.arange(VISIBILITIES, dtype=jnp.int32)
    facet_index = position // VIS_DEV % N_FACET
    top = jnp.where(facet_index == N_FACET - 1, facet_cols - KW + 1, facet_cols)
    offset = jax.random.randint(key, (VISIBILITIES,), 0, top, dtype=jnp.int32)
    return facet_index * facet_cols + offset


def touch_ends(entries, key, smallest, largest):
    dims = entries.shape
    spot = [jax.random.randint(jax.random.fold_in(key, axis), (), 0, dims[axis]) for axis in range(len(dims))]
    entries = entries.at[tuple(spot)].set(smallest)
    longest = dims.index(max(dims))
    spot[longest] = (spot[longest] + 1) % dims[longest]
    return entries.at[tuple(spot)].set(largest)


def shard_levels(stream_key, dims, cuts, low, largest):
    factor_of, own = 1.0, jax.random.fold_in(stream_key, 6)
    for dim, parts in cuts:
        heights = jnp.exp(jax.random.uniform(jax.random.fold_in(own, dim), (parts,), jnp.float32, low / len(cuts), largest / len(cuts)))
        factor_of = factor_of * jnp.repeat(heights, dims[dim] // parts).reshape([-1 if axis == dim else 1 for axis in range(len(dims))])
    return factor_of


def normal_values(own_key, shape, scale, limit, cuts=(), held_as=jnp.bfloat16):
    array = jax.random.normal(own_key, shape, jnp.float32) * scale
    if len(cuts) > 0:
        array = shard_levels(own_key, shape, cuts, -0.22, 0.18) * array
    return jnp.clip(array, min=-limit, max=limit).astype(held_as)


def setup_inputs(seed: int = 0) -> dict:
    arg_keys = jax.random.split(jax.random.key(seed), 10)
    image = jnp.clip(2.0 * jax.random.uniform(arg_keys[0], (NPIX, NPIX), jnp.float32) ** shard_levels(arg_keys[0], (NPIX, NPIX), ((0, 64), (1, 8)), -0.2, 0.2), 0.0, 2.0)
    observed = normal_values(arg_keys[1], (2, VISIBILITIES), 1.0, 6.0, ((1, 512),), jnp.float32)
    weights = jnp.clip(jnp.exp(math.log(4.0) - 2.7725887 * jax.random.uniform(arg_keys[2], (VISIBILITIES,), jnp.float32) ** shard_levels(arg_keys[2], (VISIBILITIES,), ((0, 512),), -0.2, 0.2)), 0.25, 4.0)
    row_cell = touch_ends(jax.random.randint(arg_keys[3], (VISIBILITIES,), 0, ROWS - KW + 1), jax.random.fold_in(arg_keys[3], 1), 0, ROWS - KW).astype(jnp.int32)
    col_cell = draw_col_cell(jax.random.fold_in(arg_keys[9], 71), 0)
    row_offset = touch_ends(jax.random.randint(arg_keys[5], (VISIBILITIES,), 0, OVERSAMPLE), jax.random.fold_in(arg_keys[5], 1), 0, OVERSAMPLE - 1).astype(jnp.int32)
    col_offset = touch_ends(jax.random.randint(arg_keys[6], (VISIBILITIES,), 0, OVERSAMPLE), jax.random.fold_in(arg_keys[6], 1), 0, OVERSAMPLE - 1).astype(jnp.int32)
    kernel = jnp.clip(jax.random.uniform(arg_keys[7], (OVERSAMPLE, KW), jnp.float32, 0.1, 1.0), 0.1, 1.0)
    thresholds = jnp.clip(jnp.exp(jax.random.uniform(arg_keys[8], (LEVELS,), jnp.float32, math.log(0.02), math.log(0.4))), 0.02, 0.4)
    return {"image": image, "observed": observed, "weights": weights, "row_cell": row_cell, "col_cell": col_cell, "row_offset": row_offset, "col_offset": col_offset, "kernel": kernel, "thresholds": thresholds}


STEP = 0.5
SPLINE = (0.0625, 0.25, 0.375, 0.25, 0.0625)

def row_tables(first_row, count, total, uv_rows):
    rows = first_row + jnp.arange(count, dtype=jnp.int32)
    freqs = total // 8 + jnp.arange(uv_rows, dtype=jnp.int32)
    turn = freqs[:, None] * rows[None, :] % total
    angle = 2.0 * math.pi / total * turn.astype(jnp.float32)
    return (jnp.cos(angle), jnp.sin(angle))

def grid_block(table, kernel, row_cell, col_cell, row_offset, col_offset, observed, weights):
    strip_rows = table.shape[1] // 2
    width = kernel.shape[1]
    taps = jnp.arange(width, dtype=jnp.int32)
    options = jnp.arange(kernel.shape[0], dtype=jnp.int32)
    row_pick = (row_offset[:, None] == options[None, :]).astype(kernel.dtype)
    col_pick = (col_offset[:, None] == options[None, :]).astype(kernel.dtype)
    row_taps = jnp.dot(row_pick, kernel, precision=lax.Precision.HIGHEST)
    col_taps = jnp.dot(col_pick, kernel, precision=lax.Precision.HIGHEST)
    distance = jnp.arange(strip_rows, dtype=jnp.int32)[None, :] - row_cell[:, None]
    row_weight = lax.optimization_barrier(jnp.sum((distance[:, :, None] == taps[None, None, :]).astype(kernel.dtype) * row_taps[:, None, :], axis=2))
    columns = col_cell[:, None] + taps[None, :]
    picked = table[columns]
    folded = jnp.einsum('bc,bcr->br', col_taps, picked, precision=lax.Precision.HIGHEST)
    model_re = lax.optimization_barrier(jnp.sum(folded[:, :strip_rows] * row_weight, axis=1))
    model_im = lax.optimization_barrier(jnp.sum(folded[:, strip_rows:] * row_weight, axis=1))
    misfit_re = weights * (model_re - observed[0])
    misfit_im = weights * (model_im - observed[1])
    spread = jnp.concatenate([row_weight * misfit_re[:, None], row_weight * misfit_im[:, None]], axis=1)
    values = col_taps[:, :, None] * spread[:, None, :]
    return (columns.reshape(-1), values.reshape(-1, 2 * strip_rows))

def smooth(coarse, dilation):
    margin = 2 * dilation
    padded = jnp.pad(coarse, ((margin, margin), (margin, margin)))
    row_count, col_count = coarse.shape
    across = jnp.zeros((padded.shape[0], col_count), coarse.dtype)
    for tap_index in range(5):
        begin = tap_index * dilation
        across = across + SPLINE[tap_index] * padded[:, begin:begin + col_count]
    total = jnp.zeros_like(coarse)
    for tap_index in range(5):
        begin = tap_index * dilation
        total = total + SPLINE[tap_index] * across[begin:begin + row_count, :]
    return total

def reference(image, observed, weights, row_cell, col_cell, row_offset, col_offset, kernel, thresholds):
    root = math.sqrt(NPIX)
    row_cos, row_sin = row_tables(0, NPIX, NPIX, ROWS)
    part_re = jnp.dot(row_cos, image, precision=lax.Precision.HIGHEST) / root
    part_im = -jnp.dot(row_sin, image, precision=lax.Precision.HIGHEST) / root
    spectrum = jnp.fft.fft(part_re + 1j * part_im, axis=1, norm='ortho')
    table = jnp.concatenate([jnp.real(spectrum).T, jnp.imag(spectrum).T], axis=1).astype(jnp.float32)
    block = math.gcd(VISIBILITIES, 65536)
    count = VISIBILITIES // block
    pieces = (row_cell.reshape(count, block), col_cell.reshape(count, block), row_offset.reshape(count, block), col_offset.reshape(count, block), jnp.moveaxis(observed.reshape(2, count, block), 1, 0), weights.reshape(count, block))

    def accumulate(grid, piece):
        columns, values = grid_block(table, kernel, piece[0], piece[1], piece[2], piece[3], piece[4], piece[5])
        return (grid.at[columns].add(values), None)
    grid, unused = lax.scan(accumulate, jnp.zeros((NPIX, 2 * ROWS), jnp.float32), pieces)
    totals = grid[:, :ROWS].T + 1j * grid[:, ROWS:].T
    back = jnp.fft.ifft(totals, axis=1, norm='ortho')
    scale = NPIX / (4.0 * math.sqrt(VISIBILITIES)) / root
    gradient = (jnp.dot(row_cos.T, jnp.real(back), precision=lax.Precision.HIGHEST) - jnp.dot(row_sin.T, jnp.imag(back), precision=lax.Precision.HIGHEST)) * scale
    coarse = image - STEP * gradient
    kept = jnp.zeros_like(coarse)
    for level_index in range(LEVELS):
        smoother = smooth(coarse, 2 ** level_index)
        detail = coarse - smoother
        kept = kept + detail - jnp.clip(detail, -thresholds[level_index], thresholds[level_index])
        coarse = smoother
    return jax.nn.relu(kept + coarse)
```

```python
import functools
import math

import jax
import jax.numpy as jnp
import numpy as np
from jax import lax
from jax.experimental import pallas as pl
from jax.experimental.pallas import tpu as pltpu
from jax.sharding import PartitionSpec as P

NPIX = 16384
ROWS = 16
BAND = 256
COLS = 2048
Z = 16
W = 4
F = 8
KW = 8
VDEV = 2048
TAPS = 15
STEP = 0.5
SPLINE = (0.0625, 0.25, 0.375, 0.25, 0.0625)
MESH = pl.DeviceIdType.MESH
HI = lax.Precision.HIGHEST
f32 = jnp.float32
bf16 = jnp.bfloat16


def turn(value, period):
    return 2.0 * np.pi * (np.asarray(value, np.int64) % period).astype(np.float64) / period


def forward_mix():
    f = np.arange(F)[:, None, None]
    l = (2 * np.arange(W)[:, None] + np.arange(2)[None, :])[None]
    f, l = np.broadcast_arrays(f, l)

    def row(j, b, im):
        ang = turn(8 * f * j + 8 * l * b + l * j, 64)
        c, s = np.cos(ang), np.sin(ang)
        pair = (c, s) if im == 0 else (-s, c)
        return np.stack(pair, axis=2).reshape(-1)

    def quarter(j, b, im):
        return row(j, b, 1) if im == 0 else -row(j, b, 0)

    out = np.zeros((W, 96, 128))
    for w in range(W):
        rows = []
        for b_lo in range(4):
            for kind in (row, quarter):
                for im in range(2):
                    for j2 in range(2):
                        for h in range(2):
                            rows.append(kind(2 * w + j2, 4 * h + b_lo, im))
        for kind in (row, quarter):
            for im in range(2):
                for j in range(8):
                    rows.append(kind(j, 0, im))
        out[w] = np.stack(rows)
    return out.astype(np.float32)


def forward_freqs():
    out = np.zeros((W, 48), np.int32)
    for w in range(W):
        rows = [
            8 * (4 * h + b_lo) + 2 * w + j2
            for b_lo in range(4)
            for _ in range(2)
            for j2 in range(2)
            for h in range(2)
        ]
        rows += [2048 + j for _ in range(2) for j in range(8)]
        out[w] = rows
    return out


def forward_last():
    m = np.arange(256)[:, None]
    a = np.tile(np.arange(32), 4)[None, :]
    ang = turn(m * a, 256)
    return (np.concatenate([np.cos(ang), np.sin(ang)], axis=0) / 128.0).astype(np.float32)


def backward_first():
    t = np.arange(256)[:, None]
    m = np.arange(256)[None, :]
    ang = turn(t * m, 256)
    return np.concatenate([np.cos(ang), np.sin(ang)], axis=0).astype(np.float32)


def backward_order():
    return [
        (2 * w + j2, 4 * h + b_lo, im)
        for b_lo in range(4)
        for w in range(W)
        for im in range(2)
        for j2 in range(2)
        for h in range(2)
    ]


def backward_twist():
    freq = np.array([j + 8 * b for j, b, _ in backward_order()])[:, None]
    ang = turn(freq * np.arange(256)[None, :], NPIX)
    return np.stack([np.cos(ang), np.sin(ang)]).astype(np.float32)


def backward_mix(scale):
    order = backward_order()
    j = np.array([o[0] for o in order])
    b = np.array([o[1] for o in order])
    im_in = np.array([o[2] for o in order])

    def row(f, l, im):
        ang = turn(8 * f * j + 8 * l * b + l * j, 64)
        c, s = np.cos(ang), np.sin(ang)
        if im == 0:
            return np.where(im_in == 0, c, -s)
        return np.where(im_in == 0, s, c)

    out = np.zeros((F * W, 24, 128))
    for f in range(F):
        for w in range(W):
            here = out[f * W + w]
            for copy in range(2):
                for im in range(2):
                    for l1 in range(2):
                        here[copy * 4 + im * 2 + l1] = row(f, 2 * w + l1, im)
            for im in range(2):
                here[8 + im] = row(f, 8, im)
                here[16 + im] = row(f, -1, im)
    return (out * scale).astype(np.float32)


def split(x):
    hi = x.astype(bf16)
    return hi, (x - hi.astype(f32)).astype(bf16)


def split_host(x):
    hi = x.astype(jnp.bfloat16)
    lo = (x - hi.astype(np.float64)).astype(jnp.bfloat16)
    return hi, lo


def row_waves():
    u = np.arange(ROWS)[:, None] + NPIX // 8
    ang = turn(u * np.arange(-8, BAND + 8)[None, :], NPIX)
    return np.concatenate([np.cos(ang), -np.sin(ang)], axis=0)


def smooth_rows(x, dilation):
    out = np.zeros_like(x)
    for s, weight in zip(range(-2, 3), SPLINE):
        out += weight * np.roll(x, -s * dilation, axis=1)
    return out


def gradient_tables():
    out = np.zeros((3, 3, BAND, 96), jnp.bfloat16)
    base = row_waves()
    inside = np.ones((3, BAND + 16))
    inside[0, :8] = 0
    inside[2, BAND + 8 :] = 0
    for edge in range(3):
        level = base
        for step in range(3):
            if step:
                level = smooth_rows(level * inside[edge], 2 ** (step - 1))
            hi, lo = split_host(level[:, 8 : 8 + BAND].T)
            out[edge, step] = np.concatenate([hi, hi, lo], axis=1)
    return out


def dot(a, b, precision=None):
    return jnp.dot(a, b, preferred_element_type=f32, precision=precision)


def position():
    v = lax.axis_index("vis")
    return v, v // W, v % W, lax.axis_index("facet")


def local_peer(v, z, w, f, d):
    return (z * W + (w + d) % W, f)


def depth_peer(v, z, w, f, d):
    return (((z + d) % Z) * W + w, f)


def plane_peer(v, z, w, f, d):
    return (z * W + (w + d % W) % W, (f + d // W) % F)


def meet(pos, depth, plane, extra=()):
    barrier = pltpu.get_barrier_semaphore()

    def greet(peer):
        pl.semaphore_signal(barrier, inc=1, device_id=peer, device_id_type=MESH)

    def along(count, where):
        def body(d, carry):
            greet(where(*pos, d))
            return carry

        lax.fori_loop(1, count, body, 0)

    along(Z, depth)
    along(F * W, plane)
    for peer in extra:
        greet(peer)
    return barrier, (Z - 1) + (F * W - 1) + len(extra)


def exchange(pos, count, where, src, dst, sems):
    def copy(d):
        return pltpu.make_async_remote_copy(
            src_ref=src(d),
            dst_ref=dst(d),
            send_sem=sems.at[0, d],
            recv_sem=sems.at[1, d],
            device_id=where(*pos, d),
            device_id_type=MESH,
        )

    def start():
        def body(d, carry):
            copy(d).start()
            return carry

        lax.fori_loop(1, count, body, 0)

    def wait_recv():
        def body(d, carry):
            copy(d).wait_recv()
            return carry

        lax.fori_loop(1, count, body, 0)

    def wait_send():
        def body(d, carry):
            copy(d).wait_send()
            return carry

        lax.fori_loop(1, count, body, 0)

    return start, wait_recv, wait_send


def rows8(ref, slot):
    return ref.at[pl.ds(pl.multiple_of(slot * 8, 8), 8)]


def rows128(ref, slot):
    return ref.at[pl.ds(pl.multiple_of(slot * 128, 128), 128)]


def forward_kernel(
    image, waves, mix, twist, last,
    x_out, rim_out, left_out, right_out, top_out, bottom_out,
    parts, near, summed, far, mine, gathered, block, blocks, rim_row, rims,
    pack, left, right, top, bottom,
    near_sem, far_sem, plane_sem, depth_sem, rim_sem, spread_sem, halo_sem,
):
    pos = position()
    v, z, w, f = pos
    vs = ((v + Z * W - 1) % (Z * W), v, (v + 1) % (Z * W))
    fs = ((f + F - 1) % F, f, (f + 1) % F)
    ring = [(vs[i], fs[k]) for i in range(3) for k in range(3) if (i, k) != (1, 1)]
    barrier, count = meet(pos, depth_peer, plane_peer, ring)

    table = waves[...]
    table_hi, table_lo = split(table)
    both = jnp.concatenate([table_hi, table_lo], axis=0)
    for tile in range(8):
        lanes = pl.ds(tile * 256, 256)
        hi, lo = split(image[:, lanes])
        first = dot(both, hi)
        value = first[:32] + first[32:] + dot(table_hi, lo)
        for half in range(2):
            c = (tile % 2) * 2 + half
            for im in range(2):
                parts[pl.ds((tile // 2) * 128 + im * 4 + c, 16, stride=8), :] = value[
                    im * 16 : im * 16 + 16, half * 128 : half * 128 + 128
                ]
    pack[0] = jnp.transpose(image[:, 0:128])[0:8]
    pack[1] = jnp.transpose(image[:, COLS - 128 : COLS])[120:128]
    pl.semaphore_wait(barrier, count)

    start, recv, send = exchange(
        pos, W, local_peer,
        lambda d: rows128(parts, (w + d) % W), lambda d: rows128(near, d - 1), near_sem,
    )
    start()
    halo = []

    def halo_copy(src, dst, peer):
        halo.append(
            pltpu.make_async_remote_copy(
                src_ref=src, dst_ref=dst, send_sem=halo_sem.at[0, len(halo)],
                recv_sem=halo_sem.at[1, len(halo)], device_id=peer, device_id_type=MESH,
            )
        )
        halo[-1].start()

    halo_copy(image.at[pl.ds(0, 8)], bottom, (vs[0], fs[1]))
    halo_copy(image.at[pl.ds(BAND - 8, 8)], top, (vs[2], fs[1]))
    halo_copy(pack.at[0], right.at[:, pl.ds(128, 256)], (vs[1], fs[0]))
    halo_copy(pack.at[1], left.at[:, pl.ds(128, 256)], (vs[1], fs[2]))
    halo_copy(pack.at[0, :, pl.ds(0, 128)], right.at[:, pl.ds(384, 128)], (vs[0], fs[0]))
    halo_copy(pack.at[0, :, pl.ds(128, 128)], right.at[:, pl.ds(0, 128)], (vs[2], fs[0]))
    halo_copy(pack.at[1, :, pl.ds(0, 128)], left.at[:, pl.ds(384, 128)], (vs[0], fs[2]))
    halo_copy(pack.at[1, :, pl.ds(128, 128)], left.at[:, pl.ds(0, 128)], (vs[2], fs[2]))
    recv()
    summed[...] = (
        (parts[pl.ds(pl.multiple_of(w * 128, 128), 128), :] + near[0:128])
        + (near[128:256] + near[256:384])
    )
    sends = [send]

    start, recv, send = exchange(
        pos, Z, depth_peer,
        lambda d: rows8(summed, (z + d) % Z), lambda d: rows8(far, d - 1), far_sem,
    )
    start()
    recv()
    sends.append(send)
    total = summed[pl.ds(pl.multiple_of(z * 8, 8), 8), :]
    for d in range(Z - 1):
        total = total + far[d * 8 : d * 8 + 8]
    mine[...] = total

    own = f * W + w
    start, recv, send = exchange(
        pos, F * W, plane_peer,
        lambda d: mine, lambda d: rows8(gathered, own), plane_sem,
    )
    start()
    gathered[pl.ds(pl.multiple_of(own * 8, 8), 8), :] = total
    sends.append(send)
    recv()

    wide = jnp.concatenate(
        [gathered[pl.ds(0, 128, stride=2), :], gathered[pl.ds(1, 128, stride=2), :]], axis=1
    )
    mixed = dot(mix[w], wide, HI)
    cos, sin = twist[0], twist[1]
    turned_a, turned_b = [], []
    for part in range(5):
        size = 16 if part == 4 else 8
        a = mixed[part * 16 : part * 16 + size]
        b = mixed[part * 16 + size : part * 16 + 2 * size]
        c = cos[part * 8 : part * 8 + size]
        s = sin[part * 8 : part * 8 + size]
        turned_a.append(a * c + b * s)
        turned_b.append(b * c - a * s)
    turned = jnp.concatenate(
        [jnp.concatenate(turned_a, axis=0), jnp.concatenate(turned_b, axis=0)], axis=1
    )
    spec = dot(turned, last[...], HI)
    group = lax.broadcasted_iota(jnp.int32, (8, 128), 1) // 32
    value = spec[0:8]
    for b_lo in range(1, 4):
        value = jnp.where(group == b_lo, spec[b_lo * 8 : b_lo * 8 + 8], value)
    block[...] = value
    diagonal = lax.broadcasted_iota(jnp.int32, (16, 128), 0) == lax.broadcasted_iota(
        jnp.int32, (16, 128), 1
    )
    edge = jnp.where(diagonal, jnp.broadcast_to(spec[32:48, 0:1], (16, 128)), 0.0)
    rim_row[...] = jnp.sum(edge, axis=0, keepdims=True)

    start, recv, send = exchange(
        pos, Z, depth_peer,
        lambda d: block, lambda d: rows8(blocks, w * Z + z), depth_sem,
    )
    start()
    rim_start, rim_recv, rim_send = exchange(
        pos, Z, depth_peer, lambda d: rim_row, lambda d: rims.at[z], rim_sem,
    )
    rim_start()
    blocks[pl.ds(pl.multiple_of((w * Z + z) * 8, 8), 8), :] = value
    rims[z] = rim_row[...]
    sends += [send, rim_send]
    recv()

    start, recv, send = exchange(
        pos, W, local_peer,
        lambda d: rows128(blocks, w), lambda d: rows128(blocks, w), spread_sem,
    )
    start()
    rim_recv()
    for copy in halo:
        copy.wait()
    left_out[...] = left[...]
    right_out[...] = right[...]
    top_out[...] = top[...]
    bottom_out[...] = bottom[...]
    sends.append(send)
    recv()
    x_out[...] = blocks[...]
    for r in range(16):
        rim_out[r : r + 1, :] = rims[r]
    for send in sends:
        send()


def grid_kernel(
    x, rim, kernel_t, observed, weights, row_cell, col_cell, row_offset, col_offset,
    g_out, edge_out,
    table_hi, table_lo, pick, values_hi, values_lo,
):
    first_col = lax.axis_index("facet") * COLS
    lane = lax.broadcasted_iota(jnp.int32, (32, 256), 1)
    lane_half = lax.broadcasted_iota(jnp.int32, (16, 128), 1)

    for j in range(8):
        w, j2 = j // 2, j % 2
        both = []
        for im in range(2):
            halves = [
                x[pl.ds(w * 128 + im * 4 + j2 * 2 + h, 16, stride=8), :] for h in range(2)
            ]
            both.append(jnp.concatenate(halves, axis=1))
        tile = jnp.concatenate(both, axis=0)
        hi, lo = split(tile)
        table_hi[j * 32 : j * 32 + 32, :] = hi
        table_lo[j * 32 : j * 32 + 32, :] = lo
        if j < 7:
            beyond = jnp.concatenate(
                [
                    jnp.broadcast_to(rim[:, im * 8 + j : im * 8 + j + 1], (16, 256))
                    for im in range(2)
                ],
                axis=0,
            )
            once = pltpu.roll(tile, 224, 1)
            twice = pltpu.roll(once, 255, 1)
            moved = jnp.where(lane < 224, once, jnp.where(lane == 255, beyond, twice))
            hi, lo = split(moved)
            table_hi[(j + 8) * 32 : (j + 9) * 32, :] = hi
            table_lo[(j + 8) * 32 : (j + 9) * 32, :] = lo

    taps = kernel_t[...]
    o_of = lax.broadcasted_iota(jnp.int32, (16, 256), 1) // 16
    s_of = lax.broadcasted_iota(jnp.int32, (16, 256), 1) % 16
    rep = (lax.broadcasted_iota(jnp.int32, (16, 256), 0) == o_of).astype(f32)
    spread = dot(taps, rep, HI)
    padded = jnp.concatenate([spread, jnp.zeros((8, 256), f32)], axis=0)
    tap_table = jnp.where(s_of == 0, padded, 0.0)
    for s in range(1, 9):
        tap_table = jnp.where(s_of == s, pltpu.roll(padded, s, 0), tap_table)
    tap_hi, tap_lo = split(tap_table)
    tap_both = jnp.concatenate([tap_hi, tap_lo], axis=0)

    down = lax.broadcasted_iota(jnp.int32, (256, 256), 0)

    def onehot(index):
        return jnp.where(down == index, 1.0, 0.0).astype(bf16)

    def visit(step, carry):
        lanes = pl.ds(pl.multiple_of(step * 256, 256), 256)
        col = col_cell[:, lanes] - first_col
        q = col // 8
        chosen = onehot((q % 8) * 32 + q // 8)
        pick[:, lanes] = chosen
        col_taps = dot(tap_both, onehot(col_offset[:, lanes] * 16 + col % 8))
        col_taps = col_taps[:16] + col_taps[16:]
        row_taps = dot(tap_both, onehot(row_offset[:, lanes] * 16 + row_cell[:, lanes]))
        row_taps = row_taps[:16] + row_taps[16:]
        picked = dot(table_hi[...], chosen) + dot(table_lo[...], chosen)
        folded = picked[0:32] * col_taps[0:1]
        for d in range(1, TAPS):
            folded = folded + picked[d * 32 : d * 32 + 32] * col_taps[d : d + 1]
        misfit = []
        for im in range(2):
            model = jnp.sum(folded[im * 16 : im * 16 + 16] * row_taps, axis=0, keepdims=True)
            misfit.append(
                row_taps * (weights[:, lanes] * (model - observed[im : im + 1, lanes]))
            )
        fan = jnp.concatenate(misfit, axis=0)
        for d in range(TAPS):
            hi, lo = split(fan * col_taps[d : d + 1])
            values_hi[d * 32 : d * 32 + 32, lanes] = hi
            values_lo[d * 32 : d * 32 + 32, lanes] = lo
        return carry

    lax.fori_loop(0, VDEV // 256, visit, 0)

    def scatter(values):
        return lax.dot_general(
            values[...], pick[...], (((1,), (1,)), ((), ())), preferred_element_type=f32
        )

    grid = scatter(values_hi) + scatter(values_lo)
    edge = [jnp.zeros((16, 128), f32)]
    for j in range(8):
        w, j2 = j // 2, j % 2
        tile = grid[j * 32 : j * 32 + 32]
        if j < 7:
            over = grid[(j + 8) * 32 : (j + 9) * 32]
            once = pltpu.roll(over, 32, 1)
            twice = pltpu.roll(once, 1, 1)
            tile = tile + jnp.where(lane >= 32, once, jnp.where(lane == 0, 0.0, twice))
            for im in range(2):
                last = over[im * 16 : im * 16 + 16, 255:256]
                edge.append(
                    jnp.where(lane_half == im * 8 + j, jnp.broadcast_to(last, (16, 128)), 0.0)
                )
        for im in range(2):
            for h in range(2):
                g_out[pl.ds(w * 128 + im * 4 + j2 * 2 + h, 16, stride=8), :] = tile[
                    im * 16 : im * 16 + 16, h * 128 : h * 128 + 128
                ]
    edge_out[...] = functools.reduce(jnp.add, edge)


def rotate(x, sign):
    groups = x.shape[0] // 8
    out = []
    for g in range(groups):
        out.append(pltpu.roll(x[g * 8 : g * 8 + 8], 4, 0) * sign)
    return jnp.concatenate(out, axis=0)


def backward_kernel(
    g, edge, first, twist, mix,
    b_out, margin_out,
    near, near_edge, summed, summed_edge, far, far_edge, mine, mine_edge,
    gathered, edges, block, blocks, margin, margins,
    near_sem, near_edge_sem, far_sem, far_edge_sem, plane_sem, edge_sem, depth_sem, margin_sem,
    spread_sem,
):
    pos = position()
    v, z, w, f = pos
    barrier, count = meet(pos, depth_peer, plane_peer)
    pl.semaphore_wait(barrier, count)

    start, recv, send = exchange(
        pos, W, local_peer,
        lambda d: rows128(g, (w + d) % W), lambda d: rows128(near, d - 1), near_sem,
    )
    start()
    edge_start, edge_recv, edge_send = exchange(
        pos, W, local_peer, lambda d: edge, lambda d: near_edge.at[d - 1], near_edge_sem,
    )
    edge_start()
    sends = [send, edge_send]
    recv()
    summed[...] = (
        (g[pl.ds(pl.multiple_of(w * 128, 128), 128), :] + near[0:128])
        + (near[128:256] + near[256:384])
    )
    start, recv, send = exchange(
        pos, Z, depth_peer,
        lambda d: rows8(summed, (z + d) % Z), lambda d: rows8(far, d - 1), far_sem,
    )
    start()
    edge_recv()
    edge_sum = edge[...] + near_edge[0] + near_edge[1] + near_edge[2]
    for r in range(16):
        summed_edge[r] = edge_sum[r : r + 1]
    edge_start, edge_recv, edge_send = exchange(
        pos, Z, depth_peer,
        lambda d: summed_edge.at[(z + d) % Z], lambda d: far_edge.at[d - 1], far_edge_sem,
    )
    edge_start()
    sends += [send, edge_send]
    recv()
    total = summed[pl.ds(pl.multiple_of(z * 8, 8), 8), :]
    for d in range(Z - 1):
        total = total + far[d * 8 : d * 8 + 8]
    mine[...] = total

    own = f * W + w
    start, recv, send = exchange(
        pos, F * W, plane_peer,
        lambda d: mine, lambda d: rows8(gathered, own), plane_sem,
    )
    start()
    gathered[pl.ds(pl.multiple_of(own * 8, 8), 8), :] = total
    edge_recv()
    edge_total = summed_edge[z]
    for d in range(Z - 1):
        edge_total = edge_total + far_edge[d]
    mine_edge[...] = edge_total

    def facet_peer(v, z, w, f, d):
        return (v, (f + d) % F)

    edge_start, edge_recv, edge_send = exchange(
        pos, F, facet_peer, lambda d: mine_edge, lambda d: edges.at[f], edge_sem,
    )
    edge_start()
    edges[f] = edge_total
    sends += [send, edge_send]
    edge_recv()
    recv()

    row_index = lax.broadcasted_iota(jnp.int32, (32, 128), 0)
    lane = lax.broadcasted_iota(jnp.int32, (32, 128), 1)
    target = ((row_index // 4) % 2) * 8 + 2 * (row_index // 8) + (row_index // 2) % 2
    wanted = (lane == target) & (row_index % 2 == 0)
    tiles = []
    for facet in range(F):
        tile = gathered[facet * 32 : facet * 32 + 32]
        if facet:
            spill = jnp.where(wanted, jnp.broadcast_to(edges[facet - 1], (32, 128)), 0.0)
            column = jnp.sum(spill, axis=1, keepdims=True)
            tile = tile + jnp.where(lane == 0, jnp.broadcast_to(column, (32, 128)), 0.0)
        tiles.append(tile)
    group = lane // 32
    moved = [
        [tile if s == 0 else pltpu.roll(tile, 32 * s, 1) for s in range(4)] for tile in tiles
    ]
    rows = []
    for b_lo in range(4):
        halves = []
        for half in range(2):
            value = moved[half * 4][(0 - b_lo) % 4]
            for k in range(1, 4):
                value = jnp.where(group == k, moved[half * 4 + k][(k - b_lo) % 4], value)
            halves.append(value)
        rows.append(jnp.concatenate(halves, axis=1))
    stack = jnp.concatenate(rows, axis=0)
    sign = jnp.where(lax.broadcasted_iota(jnp.int32, (8, 256), 0) < 4, -1.0, 1.0)
    operand = jnp.concatenate([stack, rotate(stack, sign)], axis=1)
    spun = dot(operand, first[...], HI)
    spun = spun * twist[0] + rotate(spun, sign) * twist[1]
    out = dot(mix[own], spun, HI)
    top = lax.broadcasted_iota(jnp.int32, (8, 128), 0) < 4
    value = jnp.where(top, out[0:8, 0:128], out[0:8, 128:256])
    block[...] = value
    low = lax.broadcasted_iota(jnp.int32, (8, 128), 1) < 64
    sides = jnp.where(low, out[8:16, 0:128], out[16:24, 128:256])
    margin[...] = sides[0:2]

    start, recv, send = exchange(
        pos, Z, depth_peer,
        lambda d: block, lambda d: rows8(blocks, w * Z + z), depth_sem,
    )
    start()
    margin_start, margin_recv, margin_send = exchange(
        pos, Z, depth_peer, lambda d: margin, lambda d: margins.at[z], margin_sem,
    )
    margin_start()
    blocks[pl.ds(pl.multiple_of((w * Z + z) * 8, 8), 8), :] = value
    margins[z] = margin[...]
    sends += [send, margin_send]
    recv()
    start, recv, send = exchange(
        pos, W, local_peer,
        lambda d: rows128(blocks, w), lambda d: rows128(blocks, w), spread_sem,
    )
    start()
    margin_recv()
    sends.append(send)
    for r in range(16):
        for im in range(2):
            margin_out[im * 16 + r : im * 16 + r + 1, :] = margins[r, im : im + 1, :]
    recv()
    b_out[...] = blocks[...]
    for send in sends:
        send()


def weigh(x, dilation, axis):
    n = x.shape[axis]
    near = pltpu.roll(x, dilation, axis) + pltpu.roll(x, n - dilation, axis)
    wide = pltpu.roll(x, 2 * dilation, axis) + pltpu.roll(x, n - 2 * dilation, axis)
    return SPLINE[2] * x + (SPLINE[1] * near + SPLINE[0] * wide)


EXT = COLS + 256
TALL = BAND + 16


def smooth_kernel(image, left, right, top, bottom, one, two, ext, across):
    v = lax.axis_index("vis")
    f = lax.axis_index("facet")
    low_row = jnp.where(v == 0, 8, 0)
    high_row = jnp.where(v == Z * W - 1, BAND + 8, TALL)
    low_col = jnp.where(f == 0, 128, 0)
    high_col = jnp.where(f == F - 1, COLS + 128, EXT)
    ext[8 : 8 + BAND, 128 : 128 + COLS] = image[...]
    ext[0:8, 128 : 128 + COLS] = jnp.where(low_row == 0, top[...], 0.0)
    ext[BAND + 8 : TALL, 128 : 128 + COLS] = jnp.where(high_row == TALL, bottom[...], 0.0)
    tall = lax.broadcasted_iota(jnp.int32, (TALL, 128), 0)
    rows_in = (tall >= low_row) & (tall < high_row)
    side = jnp.concatenate([jnp.zeros((120, 512), f32), left[...]], axis=0)
    side = jnp.transpose(side)[120 : 120 + TALL]
    ext[:, 0:128] = jnp.where(rows_in & (low_col == 0), side, 0.0)
    side = jnp.concatenate([right[...], jnp.zeros((120, 512), f32)], axis=0)
    side = jnp.transpose(side)[120 : 120 + TALL]
    ext[:, EXT - 128 : EXT] = jnp.where(rows_in & (high_col == EXT), side, 0.0)

    def level(dilation, out):
        def columns(step, carry):
            rows = pl.ds(pl.multiple_of(step * 8, 8), 8)
            across[rows, :] = weigh(ext[rows, :], dilation, 1)
            return carry

        lax.fori_loop(0, TALL // 8, columns, 0)

        def down(step, carry):
            lanes = pl.ds(pl.multiple_of(step * 128, 128), 128)
            value = weigh(across[:, lanes], dilation, 0)
            col = lax.broadcasted_iota(jnp.int32, (TALL, 128), 1) + step * 128
            inside = rows_in & (col >= low_col) & (col < high_col)
            ext[:, lanes] = jnp.where(inside, value, 0.0)
            return carry

        lax.fori_loop(0, EXT // 128, down, 0)
        out[...] = ext[8 : 8 + BAND, 128 : 128 + COLS]

    level(1, one)
    level(2, two)


def final_kernel(image, one, two, b, margin, phase, waves, thresholds, out):
    v = lax.axis_index("vis")
    f = lax.axis_index("facet")
    edge = jnp.where(v == 0, 0, jnp.where(v == Z * W - 1, 2, 1))
    parts = []
    for im in range(2):
        tiles = [margin[im * 16 : im * 16 + 16, :]]
        for tile in range(16):
            w, l1, mh = tile // 4, (tile // 2) % 2, tile % 2
            tiles.append(b[pl.ds(w * 128 + mh * 4 + im * 2 + l1, 16, stride=8), :])
        tiles.append(margin[im * 16 : im * 16 + 16, :])
        parts.append(jnp.concatenate(tiles, axis=1))
    cos, sin = phase[0:16, 0:1], phase[16:32, 0:1]
    col = lax.broadcasted_iota(jnp.int32, (32, EXT), 1)
    low_col = jnp.where(f == 0, 128, 122)
    high_col = jnp.where(f == F - 1, COLS + 128, COLS + 134)
    inside = (col >= low_col) & (col < high_col)
    back = jnp.concatenate(
        [parts[0] * cos - parts[1] * sin, parts[1] * cos + parts[0] * sin], axis=0
    )
    levels = [jnp.where(inside, back, 0.0)]
    for dilation in (1, 2):
        levels.append(jnp.where(inside, weigh(levels[-1], dilation, 1), 0.0))
    operands = []
    for value in levels:
        hi, lo = split(value[:, 128 : 128 + COLS])
        operands.append(jnp.concatenate([hi, lo, hi], axis=0))
    for tile in range(COLS // 256):
        lanes = slice(tile * 256, tile * 256 + 256)
        c0 = image[:, lanes] - dot(waves[edge, 0], operands[0][:, lanes])
        c1 = one[:, lanes] - dot(waves[edge, 1], operands[1][:, lanes])
        c2 = two[:, lanes] - dot(waves[edge, 2], operands[2][:, lanes])
        d0, d1 = c0 - c1, c1 - c2
        t0, t1 = thresholds[0], thresholds[1]
        kept = (d0 - jnp.clip(d0, -t0, t0)) + (d1 - jnp.clip(d1, -t1, t1))
        out[:, lanes] = jnp.maximum(kept + c2, 0.0)


def vmem(count):
    return [pl.BlockSpec(memory_space=pltpu.VMEM)] * count


def sds(*shape, dtype=f32):
    return jax.ShapeDtypeStruct(shape, dtype)


LIMIT = 48 * 1024 * 1024


def call(body, outs, ins, scratch, **params):
    return pl.pallas_call(
        body,
        out_shape=outs,
        in_specs=ins,
        out_specs=jax.tree.map(lambda _: pl.BlockSpec(memory_space=pltpu.VMEM), outs),
        scratch_shapes=scratch,
        compiler_params=pltpu.CompilerParams(vmem_limit_bytes=LIMIT, **params),
    )


def pairs(count):
    return pltpu.SemaphoreType.DMA((2, count))


def on_device(
    image, observed, weights, row_cell, col_cell, row_offset, col_offset, kernel, thresholds
):
    v = lax.axis_index("vis")
    w = v % W
    f = lax.axis_index("facet")
    root = math.sqrt(NPIX)
    m = jnp.arange(256, dtype=jnp.int32)
    u = NPIX // 8 + jnp.arange(ROWS, dtype=jnp.int32)
    angle = (2.0 * math.pi / NPIX) * (u[:, None] * (v * BAND + m)[None, :] % NPIX).astype(f32)
    waves = jnp.concatenate([jnp.cos(angle), -jnp.sin(angle)], axis=0)
    freq = lax.dynamic_index_in_dim(jnp.asarray(forward_freqs()), w, 0, False) + f * COLS
    angle = (2.0 * math.pi / NPIX) * (freq[:, None] * m[None, :] % NPIX).astype(f32)
    twist = jnp.stack([jnp.cos(angle), jnp.sin(angle)])
    angle = (2.0 * math.pi / NPIX) * (u * (v * BAND) % NPIX).astype(f32)
    phase = jnp.concatenate([jnp.cos(angle), jnp.sin(angle)])
    phase = jnp.broadcast_to(phase[:, None], (32, 128))

    V = pltpu.VMEM
    x, rim, left, right, top, bottom = call(
        forward_kernel,
        [sds(512, 128), sds(16, 128), sds(8, 512), sds(8, 512), sds(8, COLS), sds(8, COLS)],
        vmem(5),
        [
            V((512, 128), f32), V((384, 128), f32), V((128, 128), f32), V((120, 128), f32),
            V((8, 128), f32), V((256, 128), f32), V((8, 128), f32), V((512, 128), f32),
            V((1, 128), f32), V((16, 1, 128), f32),
            V((2, 8, 256), f32), V((8, 512), f32), V((8, 512), f32), V((8, COLS), f32),
            V((8, COLS), f32),
            pairs(W), pairs(Z), pairs(F * W), pairs(Z), pairs(Z), pairs(W), pairs(8),
        ],
        collective_id=0, has_side_effects=True,
    )(image, waves, jnp.asarray(forward_mix()), twist, jnp.asarray(forward_last() / 128.0))
    g, edge = call(
        grid_kernel,
        [sds(512, 128), sds(16, 128)],
        vmem(9),
        [V((480, 256), bf16), V((480, 256), bf16), V((256, VDEV), bf16),
         V((480, VDEV), bf16), V((480, VDEV), bf16)],
    )(
        x, rim, kernel.T, observed, weights[None], row_cell[None], col_cell[None],
        row_offset[None], col_offset[None],
    )
    scale = STEP * NPIX / (4.0 * math.sqrt(VDEV * Z * W * F)) / root / root
    b, margin = call(
        backward_kernel,
        [sds(512, 128), sds(32, 128)],
        vmem(5),
        [
            V((384, 128), f32), V((3, 16, 128), f32), V((128, 128), f32), V((16, 1, 128), f32),
            V((120, 128), f32), V((15, 1, 128), f32), V((8, 128), f32), V((1, 128), f32),
            V((256, 128), f32), V((8, 1, 128), f32), V((8, 128), f32), V((512, 128), f32),
            V((2, 128), f32), V((16, 2, 128), f32),
            pairs(W), pairs(W), pairs(Z), pairs(Z), pairs(F * W), pairs(F), pairs(Z), pairs(Z),
            pairs(W),
        ],
        collective_id=1, has_side_effects=True,
    )(
        g, edge, jnp.asarray(backward_first()), jnp.asarray(backward_twist()),
        jnp.asarray(backward_mix(scale)),
    )
    one, two = call(
        smooth_kernel,
        [sds(BAND, COLS), sds(BAND, COLS)],
        vmem(5),
        [V((TALL, EXT), f32), V((TALL, EXT), f32)],
    )(image, left, right, top, bottom)
    return call(
        final_kernel,
        sds(BAND, COLS),
        vmem(7) + [pl.BlockSpec(memory_space=pltpu.SMEM)],
        [],
    )(image, one, two, b, margin, phase, jnp.asarray(gradient_tables()), thresholds)


def solution(mesh):
    return jax.shard_map(
        on_device,
        mesh=mesh,
        in_specs=(
            P("vis", "facet"),
            P(None, ("vis", "facet")),
            P(("vis", "facet")),
            P(("vis", "facet")),
            P(("vis", "facet")),
            P(("vis", "facet")),
            P(("vis", "facet")),
            P(),
            P(),
        ),
        out_specs=P("vis", "facet"),
        check_vma=False,
    )
```

```python
import functools
import math

import jax
import jax.numpy as jnp
import numpy as np
from jax import lax
from jax.experimental import pallas as pl
from jax.experimental.pallas import tpu as pltpu
from jax.sharding import PartitionSpec as P

NPIX = 16384
ROWS = 16
BAND = 256
COLS = 2048
Z = 16
W = 4
F = 8
KW = 8
VDEV = 2048
TAPS = 15
STEP = 0.5
SPLINE = (0.0625, 0.25, 0.375, 0.25, 0.0625)
MESH = pl.DeviceIdType.MESH
HI = lax.Precision.HIGHEST
f32 = jnp.float32
bf16 = jnp.bfloat16


def turn(value, period):
    return 2.0 * np.pi * (np.asarray(value, np.int64) % period).astype(np.float64) / period


def forward_mix():
    f = np.arange(F)[:, None, None]
    l = (2 * np.arange(W)[:, None] + np.arange(2)[None, :])[None]
    f, l = np.broadcast_arrays(f, l)

    def row(j, b, im):
        ang = turn(8 * f * j + 8 * l * b + l * j, 64)
        c, s = np.cos(ang), np.sin(ang)
        pair = (c, s) if im == 0 else (-s, c)
        return np.stack(pair, axis=2).reshape(-1)

    def quarter(j, b, im):
        return row(j, b, 1) if im == 0 else -row(j, b, 0)

    out = np.zeros((W, 96, 128))
    for w in range(W):
        rows = []
        for b_lo in range(4):
            for kind in (row, quarter):
                for im in range(2):
                    for j2 in range(2):
                        for h in range(2):
                            rows.append(kind(2 * w + j2, 4 * h + b_lo, im))
        for kind in (row, quarter):
            for im in range(2):
                for j in range(8):
                    rows.append(kind(j, 0, im))
        out[w] = np.stack(rows)
    return out.astype(np.float32)


def forward_freqs():
    out = np.zeros((W, 48), np.int32)
    for w in range(W):
        rows = [
            8 * (4 * h + b_lo) + 2 * w + j2
            for b_lo in range(4)
            for _ in range(2)
            for j2 in range(2)
            for h in range(2)
        ]
        rows += [2048 + j for _ in range(2) for j in range(8)]
        out[w] = rows
    return out


def forward_last():
    m = np.arange(256)[:, None]
    a = np.tile(np.arange(32), 4)[None, :]
    ang = turn(m * a, 256)
    return (np.concatenate([np.cos(ang), np.sin(ang)], axis=0) / 128.0).astype(np.float32)


def backward_first():
    t = np.arange(256)[:, None]
    m = np.arange(256)[None, :]
    ang = turn(t * m, 256)
    return np.concatenate([np.cos(ang), np.sin(ang)], axis=0).astype(np.float32)


def backward_order():
    return [
        (2 * w + j2, 4 * h + b_lo, im)
        for b_lo in range(4)
        for w in range(W)
        for im in range(2)
        for j2 in range(2)
        for h in range(2)
    ]


def backward_twist():
    freq = np.array([j + 8 * b for j, b, _ in backward_order()])[:, None]
    ang = turn(freq * np.arange(256)[None, :], NPIX)
    return np.stack([np.cos(ang), np.sin(ang)]).astype(np.float32)


def backward_mix(scale):
    order = backward_order()
    j = np.array([o[0] for o in order])
    b = np.array([o[1] for o in order])
    im_in = np.array([o[2] for o in order])

    def row(f, l, im):
        ang = turn(8 * f * j + 8 * l * b + l * j, 64)
        c, s = np.cos(ang), np.sin(ang)
        if im == 0:
            return np.where(im_in == 0, c, -s)
        return np.where(im_in == 0, s, c)

    out = np.zeros((F * W, 24, 128))
    for f in range(F):
        for w in range(W):
            here = out[f * W + w]
            for copy in range(2):
                for im in range(2):
                    for l1 in range(2):
                        here[copy * 4 + im * 2 + l1] = row(f, 2 * w + l1, im)
            for im in range(2):
                here[8 + im] = row(f, 8, im)
                here[16 + im] = row(f, -1, im)
    return (out * scale).astype(np.float32)


def split(x):
    hi = x.astype(bf16)
    return hi, (x - hi.astype(f32)).astype(bf16)


def split_host(x):
    hi = x.astype(jnp.bfloat16)
    lo = (x - hi.astype(np.float64)).astype(jnp.bfloat16)
    return hi, lo


def row_waves():
    u = np.arange(ROWS)[:, None] + NPIX // 8
    ang = turn(u * np.arange(-8, BAND + 8)[None, :], NPIX)
    return np.concatenate([np.cos(ang), -np.sin(ang)], axis=0)


def smooth_rows(x, dilation):
    out = np.zeros_like(x)
    for s, weight in zip(range(-2, 3), SPLINE):
        out += weight * np.roll(x, -s * dilation, axis=1)
    return out


def gradient_tables():
    out = np.zeros((3, 3, BAND, 96), jnp.bfloat16)
    base = row_waves()
    inside = np.ones((3, BAND + 16))
    inside[0, :8] = 0
    inside[2, BAND + 8 :] = 0
    for edge in range(3):
        level = base
        for step in range(3):
            if step:
                level = smooth_rows(level * inside[edge], 2 ** (step - 1))
            hi, lo = split_host(level[:, 8 : 8 + BAND].T)
            out[edge, step] = np.concatenate([hi, hi, lo], axis=1)
    return out


def dot(a, b, precision=None):
    return jnp.dot(a, b, preferred_element_type=f32, precision=precision)


def position():
    v = lax.axis_index("vis")
    return v, v // W, v % W, lax.axis_index("facet")


def band_waves():
    rows = np.arange(Z * W)[:, None] * BAND + np.arange(BAND)[None, :]
    u = NPIX // 8 + np.arange(ROWS)
    ang = turn(u[None, :, None] * rows[:, None, :], NPIX)
    return np.concatenate([np.cos(ang), -np.sin(ang)], axis=1).astype(np.float32)


def forward_twist():
    freq = np.arange(F)[:, None, None] * COLS + forward_freqs()[None]
    ang = turn(freq.reshape(F * W, 48, 1) * np.arange(256), NPIX)
    return np.stack([np.cos(ang), np.sin(ang)], axis=1).astype(np.float32)


def band_phases():
    u = NPIX // 8 + np.arange(ROWS)
    ang = turn(u[None, :] * (np.arange(Z * W)[:, None] * BAND), NPIX)
    both = np.concatenate([np.cos(ang), np.sin(ang)], axis=1)
    return np.broadcast_to(both[:, :, None], (Z * W, 32, 128)).astype(np.float32)


def loop(count, body):
    def step(i, carry):
        body(i)
        return carry

    lax.fori_loop(0, count, step, 0)


def far_first(i):
    k = (i + 1) // 2
    return 8 + k - 2 * k * (i % 2)


FACETS_FAR_FIRST = (3, 5, 1, 7, 4, 2, 6, 0)


def rows8(ref, slot):
    return ref.at[pl.ds(pl.multiple_of(slot * 8, 8), 8)]


class Links:
    def __init__(self):
        self.v, self.z, self.w, self.f = position()
        self.pending = []

    def local(self, d):
        return (self.z * W + (self.w + d) % W, self.f)

    def depth(self, d):
        return (((self.z + d) % Z) * W + self.w, self.f)

    def plane(self, df, dw):
        return (self.z * W + (self.w + dw) % W, (self.f + df) % F)

    def copy(self, src, dst, sems, slot, peer):
        return pltpu.make_async_remote_copy(
            src_ref=src, dst_ref=dst, send_sem=sems.at[0, slot], recv_sem=sems.at[1, slot],
            device_id=peer, device_id_type=MESH,
        )

    def greet(self, extra):
        barrier = pltpu.get_barrier_semaphore()

        def signal(peer):
            pl.semaphore_signal(barrier, inc=1, device_id=peer, device_id_type=MESH)

        loop(Z - 1, lambda i: signal(self.depth(far_first(i))))
        for df in FACETS_FAR_FIRST:
            first = 0 if df else 1
            loop(W - first, lambda i: signal(self.plane(df, i + first)))
        for peer in extra:
            signal(peer)
        count = (Z - 1) + (F * W - 1) + len(extra)
        return lambda: pl.semaphore_wait(barrier, count)

    def later(self, wait):
        self.pending.append(wait)

    def finish(self):
        for wait in self.pending:
            wait()

    def reduce_rows(self, parts, near, near_sem, summed, far, far_sem):
        def near_copy(row, d):
            here = ((self.w + d) % W) * Z + row
            return self.copy(
                rows8(parts, here), rows8(near, (d - 1) * Z + row), near_sem,
                (d - 1) * Z + row, self.local(d),
            )

        def far_copy(d):
            row = (self.z + d) % Z
            return self.copy(rows8(summed, row), rows8(far, d), far_sem, d, self.depth(d))

        def send_row(row):
            for d in range(1, W):
                near_copy(row, d).start()

        def sum_row(row):
            for d in range(1, W):
                near_copy(row, d).wait_recv()
            value = parts[pl.ds(pl.multiple_of((self.w * Z + row) * 8, 8), 8), :]
            for d in range(1, W):
                value = value + near[
                    pl.ds(pl.multiple_of(((d - 1) * Z + row) * 8, 8), 8), :
                ]
            summed[pl.ds(pl.multiple_of(row * 8, 8), 8), :] = value

        loop(Z - 1, lambda i: send_row((self.z + far_first(i)) % Z))
        send_row(self.z)

        def forward():
            def step(i):
                d = far_first(i)
                sum_row((self.z + d) % Z)
                far_copy(d).start()

            loop(Z - 1, step)
            sum_row(self.z)

        def result():
            loop(Z - 1, lambda i: far_copy(i + 1).wait_recv())
            value = summed[pl.ds(pl.multiple_of(self.z * 8, 8), 8), :]
            for d in range(1, Z):
                value = value + far[d * 8 : d * 8 + 8]
            return value

        def done(row):
            for d in range(1, W):
                near_copy(row, d).wait_send()

        self.later(lambda: loop(Z, done))
        self.later(lambda: loop(Z - 1, lambda i: far_copy(i + 1).wait_send()))
        return forward, result

    def share_plane(self, mine, gathered, sem):
        own = self.f * W + self.w

        def each(act):
            for df in FACETS_FAR_FIRST:
                first = 0 if df else 1
                loop(
                    W - first,
                    lambda i: act(
                        self.copy(
                            mine, rows8(gathered, own), sem, df * W + i + first,
                            self.plane(df, i + first),
                        )
                    ),
                )

        each(lambda c: c.start())
        gathered[pl.ds(pl.multiple_of(own * 8, 8), 8), :] = mine[...]
        self.later(lambda: each(lambda c: c.wait_send()))
        return lambda: each(lambda c: c.wait_recv())

    def spread(self, block, blocks, depth_sem, local_sem):
        def depth_copy(d):
            return self.copy(
                block, rows8(blocks, self.w * Z + self.z), depth_sem, d, self.depth(d)
            )

        def local_copy(row, d):
            slot = self.w * Z + row
            return self.copy(
                rows8(blocks, slot), rows8(blocks, slot), local_sem, (d - 1) * Z + row,
                self.local(d),
            )

        def pass_on(row):
            for d in range(1, W):
                local_copy(row, d).start()

        loop(Z - 1, lambda i: depth_copy(far_first(i)).start())
        blocks[pl.ds(pl.multiple_of((self.w * Z + self.z) * 8, 8), 8), :] = block[...]
        pass_on(self.z)

        def relay():
            def step(i):
                d = far_first(Z - 2 - i)
                depth_copy(d).wait_recv()
                pass_on((self.z - d + Z) % Z)

            loop(Z - 1, step)

            def arrived(row):
                for d in range(1, W):
                    local_copy(row, d).wait_recv()

            loop(Z, arrived)

        def done(row):
            for d in range(1, W):
                local_copy(row, d).wait_send()

        self.later(lambda: loop(Z - 1, lambda i: depth_copy(i + 1).wait_send()))
        self.later(lambda: loop(Z, done))
        return relay

    def each_depth(self, src, dst, sem):
        def make(d):
            return self.copy(src(d), dst(d), sem, d, self.depth(d))

        loop(Z - 1, lambda i: make(far_first(i)).start())
        self.later(lambda: loop(Z - 1, lambda i: make(i + 1).wait_send()))
        return lambda: loop(Z - 1, lambda i: make(i + 1).wait_recv())


EXT = COLS + 256
TALL = BAND + 16
CHUNKS = 4


def main_kernel(
    image, waves_all, mix_all, twist_all, last_hbm, first_hbm, turn_hbm, unmix_all,
    kernel_t, observed, weights, row_cell, col_cell, row_offset, col_offset,
    b_out, margin_out, one, two,
    ext, across, waves, mix, twist, last, first, turned_back, unmix,
    pick, col_taps_all, row_taps_all, table_hi, table_lo, values_hi, values_lo,
    parts, near, summed, far, mine, gathered, block, blocks, rim_row, rims,
    pack, left, right,
    g, edge, near2, near_edge, summed2, summed_edge, far2, far_edge, mine2, mine_edge,
    gathered2, edges, block2, blocks2, margin, margins,
    load_sem, near_sem, far_sem, plane_sem, depth_sem, local_sem, rim_sem, halo_sem,
    near_sem2, far_sem2, plane_sem2, depth_sem2, local_sem2, near_edge_sem, far_edge_sem,
    edge_sem, margin_sem,
):
    links = Links()
    v, z, w, f = links.v, links.z, links.w, links.f
    own = f * W + w
    vs = ((v + Z * W - 1) % (Z * W), v, (v + 1) % (Z * W))
    fs = ((f + F - 1) % F, f, (f + 1) % F)
    ring = [(vs[i], fs[k]) for i in range(3) for k in range(3) if (i, k) != (1, 1)]
    gathered_in = links.greet(ring)

    loads = []

    def load(src, dst):
        loads.append(pltpu.make_async_copy(src, dst, load_sem.at[len(loads)]))
        loads[-1].start()
        return loads[-1]

    span = COLS // CHUNKS
    wave_load = load(waves_all.at[v], waves)
    chunk_loads = [
        load(
            image.at[:, pl.ds(c * span, span)],
            ext.at[pl.ds(8, BAND), pl.ds(128 + c * span, span)],
        )
        for c in range(CHUNKS)
    ]
    forward_loads = [
        load(mix_all.at[w], mix), load(twist_all.at[own], twist), load(last_hbm, last),
    ]
    backward_loads = [
        load(first_hbm, first), load(turn_hbm, turned_back), load(unmix_all.at[own], unmix),
    ]

    o_of = lax.broadcasted_iota(jnp.int32, (16, 256), 1) // 16
    s_of = lax.broadcasted_iota(jnp.int32, (16, 256), 1) % 16
    rep = (lax.broadcasted_iota(jnp.int32, (16, 256), 0) == o_of).astype(f32)
    fanned = dot(kernel_t[...], rep, HI)
    padded = jnp.concatenate([fanned, jnp.zeros((8, 256), f32)], axis=0)
    tap_table = jnp.where(s_of == 0, padded, 0.0)
    for s in range(1, 9):
        tap_table = jnp.where(s_of == s, pltpu.roll(padded, s, 0), tap_table)
    tap_hi, tap_lo = split(tap_table)
    tap_both = jnp.concatenate([tap_hi, tap_lo], axis=0)
    down = lax.broadcasted_iota(jnp.int32, (256, 256), 0)
    first_col = f * COLS

    def onehot(index):
        return jnp.where(down == index, 1.0, 0.0).astype(bf16)

    def choose(step):
        lanes = pl.ds(pl.multiple_of(step * 256, 256), 256)
        col = col_cell[:, lanes] - first_col
        q = col // 8
        pick[:, lanes] = onehot((q % 8) * 32 + q // 8)
        col_taps = dot(tap_both, onehot(col_offset[:, lanes] * 16 + col % 8))
        col_taps_all[:, lanes] = col_taps[:16] + col_taps[16:]
        row_taps = dot(tap_both, onehot(row_offset[:, lanes] * 16 + row_cell[:, lanes]))
        row_taps_all[:, lanes] = row_taps[:16] + row_taps[16:]

    wave_load.wait()
    wave_hi, wave_lo = split(waves[...])
    both = jnp.concatenate([wave_hi, wave_lo], axis=0)
    for tile in range(8):
        if tile % (8 // CHUNKS) == 0:
            chunk_loads[tile // (8 // CHUNKS)].wait()
        hi, lo = split(ext[8 : 8 + BAND, 128 + tile * 256 : 384 + tile * 256])
        value = dot(both, hi)
        value = value[:32] + value[32:] + dot(wave_hi, lo)
        for half in range(2):
            c = (tile % 2) * 2 + half
            for im in range(2):
                parts[pl.ds((tile // 2) * 128 + im * 4 + c, 16, stride=8), :] = value[
                    im * 16 : im * 16 + 16, half * 128 : half * 128 + 128
                ]
    pack[0] = jnp.transpose(ext[8 : 8 + BAND, 128:256])[0:8]
    pack[1] = jnp.transpose(ext[8 : 8 + BAND, COLS : COLS + 128])[120:128]
    gathered_in()
    forward, result = links.reduce_rows(parts, near, near_sem, summed, far, far_sem)
    halo = []

    def halo_copy(src, dst, peer):
        halo.append(links.copy(src, dst, halo_sem, len(halo), peer))
        halo[-1].start()

    middle = pl.ds(128, COLS)
    halo_copy(ext.at[pl.ds(8, 8), middle], ext.at[pl.ds(BAND + 8, 8), middle], (vs[0], fs[1]))
    halo_copy(ext.at[pl.ds(BAND, 8), middle], ext.at[pl.ds(0, 8), middle], (vs[2], fs[1]))
    halo_copy(pack.at[0], right.at[:, pl.ds(128, 256)], (vs[1], fs[0]))
    halo_copy(pack.at[1], left.at[:, pl.ds(128, 256)], (vs[1], fs[2]))
    halo_copy(pack.at[0, :, pl.ds(0, 128)], right.at[:, pl.ds(384, 128)], (vs[0], fs[0]))
    halo_copy(pack.at[0, :, pl.ds(128, 128)], right.at[:, pl.ds(0, 128)], (vs[2], fs[0]))
    halo_copy(pack.at[1, :, pl.ds(0, 128)], left.at[:, pl.ds(384, 128)], (vs[0], fs[2]))
    halo_copy(pack.at[1, :, pl.ds(128, 128)], left.at[:, pl.ds(0, 128)], (vs[2], fs[2]))
    forward()

    low_row = jnp.where(v == 0, 8, 0)
    high_row = jnp.where(v == Z * W - 1, BAND + 8, TALL)
    low_col = jnp.where(f == 0, 128, 0)
    high_col = jnp.where(f == F - 1, COLS + 128, EXT)
    tall = lax.broadcasted_iota(jnp.int32, (TALL, 128), 0)
    rows_in = (tall >= low_row) & (tall < high_row)

    def assemble():
        for copy in halo:
            copy.wait()
        ext[0:8, middle] = jnp.where(low_row == 0, ext[0:8, middle], 0.0)
        bottom = pl.ds(BAND + 8, 8)
        ext[bottom, middle] = jnp.where(high_row == TALL, ext[bottom, middle], 0.0)
        side = jnp.concatenate([jnp.zeros((120, 512), f32), left[...]], axis=0)
        side = jnp.transpose(side)[120 : 120 + TALL]
        ext[:, 0:128] = jnp.where(rows_in & (low_col == 0), side, 0.0)
        side = jnp.concatenate([right[...], jnp.zeros((120, 512), f32)], axis=0)
        side = jnp.transpose(side)[120 : 120 + TALL]
        ext[:, EXT - 128 : EXT] = jnp.where(rows_in & (high_col == EXT), side, 0.0)

    def along_columns(dilation):
        def step(i):
            rows = pl.ds(pl.multiple_of(i * 8, 8), 8)
            across[rows, :] = weigh(ext[rows, :], dilation, 1)

        loop(TALL // 8, step)

    def smoothed_rows(i, dilation):
        lanes = pl.ds(pl.multiple_of(i * 128, 128), 128)
        return lanes, weigh(across[:, lanes], dilation, 0)

    def first_rows(i):
        lanes, value = smoothed_rows(i, 1)
        col = lax.broadcasted_iota(jnp.int32, (TALL, 128), 1) + i * 128
        value = jnp.where(rows_in & (col >= low_col) & (col < high_col), value, 0.0)
        ext[:, lanes] = value
        return value

    def keep_first(i):
        value = first_rows(i + 1)
        one[:, pl.ds(pl.multiple_of(i * 128, 128), 128)] = value[8 : 8 + BAND]

    def keep_second(i):
        lanes, value = smoothed_rows(i + 1, 2)
        two[:, pl.ds(pl.multiple_of(i * 128, 128), 128)] = value[8 : 8 + BAND]

    assemble()
    along_columns(1)
    total = result()
    mine[...] = total
    plane_wait = links.share_plane(mine, gathered, plane_sem)
    loop(VDEV // 256, choose)
    for copy in forward_loads:
        copy.wait()
    plane_wait()

    wide = jnp.concatenate(
        [gathered[pl.ds(0, 128, stride=2), :], gathered[pl.ds(1, 128, stride=2), :]], axis=1
    )
    mixed = dot(mix[...], wide, HI)
    cos, sin = twist[0], twist[1]
    turned_a, turned_b = [], []
    for part in range(5):
        size = 16 if part == 4 else 8
        a = mixed[part * 16 : part * 16 + size]
        b = mixed[part * 16 + size : part * 16 + 2 * size]
        c = cos[part * 8 : part * 8 + size]
        s = sin[part * 8 : part * 8 + size]
        turned_a.append(a * c + b * s)
        turned_b.append(b * c - a * s)
    turned = jnp.concatenate(
        [jnp.concatenate(turned_a, axis=0), jnp.concatenate(turned_b, axis=0)], axis=1
    )
    spec = dot(turned, last[...], HI)
    group8 = lax.broadcasted_iota(jnp.int32, (8, 128), 1) // 32
    value = spec[0:8]
    for b_lo in range(1, 4):
        value = jnp.where(group8 == b_lo, spec[b_lo * 8 : b_lo * 8 + 8], value)
    block[...] = value
    relay = links.spread(block, blocks, depth_sem, local_sem)
    diagonal = lax.broadcasted_iota(jnp.int32, (16, 128), 0) == lax.broadcasted_iota(
        jnp.int32, (16, 128), 1
    )
    corner = jnp.where(diagonal, jnp.broadcast_to(spec[32:48, 0:1], (16, 128)), 0.0)
    rim_row[...] = jnp.sum(corner, axis=0, keepdims=True)
    rim_wait = links.each_depth(lambda d: rim_row, lambda d: rims.at[z], rim_sem)
    rims[z] = rim_row[...]
    first_rows(0)
    loop(COLS // 128, keep_first)
    first_rows(EXT // 128 - 1)
    relay()
    rim_wait()

    lane = lax.broadcasted_iota(jnp.int32, (32, 256), 1)
    rim = jnp.concatenate([rims[r] for r in range(16)], axis=0)
    for j in range(8):
        both = []
        for im in range(2):
            halves = [
                blocks[pl.ds((j // 2) * 128 + im * 4 + (j % 2) * 2 + h, 16, stride=8), :]
                for h in range(2)
            ]
            both.append(jnp.concatenate(halves, axis=1))
        tile = jnp.concatenate(both, axis=0)
        hi, lo = split(tile)
        table_hi[j * 32 : j * 32 + 32, :] = hi
        table_lo[j * 32 : j * 32 + 32, :] = lo
        if j < 7:
            beyond = jnp.concatenate(
                [
                    jnp.broadcast_to(rim[:, im * 8 + j : im * 8 + j + 1], (16, 256))
                    for im in range(2)
                ],
                axis=0,
            )
            once = pltpu.roll(tile, 224, 1)
            twice = pltpu.roll(once, 255, 1)
            moved = jnp.where(lane < 224, once, jnp.where(lane == 255, beyond, twice))
            hi, lo = split(moved)
            table_hi[(j + 8) * 32 : (j + 9) * 32, :] = hi
            table_lo[(j + 8) * 32 : (j + 9) * 32, :] = lo

    def visit(step):
        lanes = pl.ds(pl.multiple_of(step * 256, 256), 256)
        chosen = pick[:, lanes]
        col_taps = col_taps_all[:, lanes]
        row_taps = row_taps_all[:, lanes]
        picked = dot(table_hi[...], chosen) + dot(table_lo[...], chosen)
        folded = picked[0:32] * col_taps[0:1]
        for d in range(1, TAPS):
            folded = folded + picked[d * 32 : d * 32 + 32] * col_taps[d : d + 1]
        misfit = []
        for im in range(2):
            model = jnp.sum(folded[im * 16 : im * 16 + 16] * row_taps, axis=0, keepdims=True)
            misfit.append(
                row_taps * (weights[:, lanes] * (model - observed[im : im + 1, lanes]))
            )
        fan = jnp.concatenate(misfit, axis=0)
        for d in range(TAPS):
            hi, lo = split(fan * col_taps[d : d + 1])
            values_hi[d * 32 : d * 32 + 32, lanes] = hi
            values_lo[d * 32 : d * 32 + 32, lanes] = lo

    loop(VDEV // 256, visit)

    def scatter(values):
        return lax.dot_general(
            values[...], pick[...], (((1,), (1,)), ((), ())), preferred_element_type=f32
        )

    grid = scatter(values_hi) + scatter(values_lo)
    lane_half = lax.broadcasted_iota(jnp.int32, (16, 128), 1)
    over_edge = [jnp.zeros((16, 128), f32)]
    for j in range(8):
        tile = grid[j * 32 : j * 32 + 32]
        if j < 7:
            over = grid[(j + 8) * 32 : (j + 9) * 32]
            once = pltpu.roll(over, 32, 1)
            twice = pltpu.roll(once, 1, 1)
            tile = tile + jnp.where(lane >= 32, once, jnp.where(lane == 0, 0.0, twice))
            for im in range(2):
                end = over[im * 16 : im * 16 + 16, 255:256]
                over_edge.append(
                    jnp.where(lane_half == im * 8 + j, jnp.broadcast_to(end, (16, 128)), 0.0)
                )
        for im in range(2):
            for h in range(2):
                g[pl.ds((j // 2) * 128 + im * 4 + (j % 2) * 2 + h, 16, stride=8), :] = tile[
                    im * 16 : im * 16 + 16, h * 128 : h * 128 + 128
                ]
    edge[...] = functools.reduce(jnp.add, over_edge)

    forward, result = links.reduce_rows(g, near2, near_sem2, summed2, far2, far_sem2)
    near_edges = [
        links.copy(edge, near_edge.at[d - 1], near_edge_sem, d, links.local(d))
        for d in range(1, W)
    ]
    for copy in near_edges:
        copy.start()
    forward()
    for copy in near_edges:
        copy.wait_recv()
        links.later(copy.wait_send)
    edge_sum = edge[...] + near_edge[0] + near_edge[1] + near_edge[2]
    for r in range(16):
        summed_edge[r] = edge_sum[r : r + 1]
    edge_wait = links.each_depth(
        lambda d: summed_edge.at[(z + d) % Z], lambda d: far_edge.at[d], far_edge_sem
    )
    along_columns(2)
    total = result()
    mine2[...] = total
    plane_wait = links.share_plane(mine2, gathered2, plane_sem2)
    edge_wait()
    edge_total = summed_edge[z]
    for d in range(1, Z):
        edge_total = edge_total + far_edge[d]
    mine_edge[...] = edge_total
    edge_copies = [
        links.copy(mine_edge, edges.at[f], edge_sem, df, links.plane(df, 0))
        for df in FACETS_FAR_FIRST[:-1]
    ]
    for copy in edge_copies:
        copy.start()
        links.later(copy.wait_send)
    edges[f] = edge_total
    loop(8, keep_second)
    for copy in backward_loads:
        copy.wait()
    for copy in edge_copies:
        copy.wait_recv()
    plane_wait()

    row_index = lax.broadcasted_iota(jnp.int32, (32, 128), 0)
    lane = lax.broadcasted_iota(jnp.int32, (32, 128), 1)
    target = ((row_index // 4) % 2) * 8 + 2 * (row_index // 8) + (row_index // 2) % 2
    wanted = (lane == target) & (row_index % 2 == 0)
    tiles = []
    for facet in range(F):
        tile = gathered2[facet * 32 : facet * 32 + 32]
        if facet:
            spill = jnp.where(wanted, jnp.broadcast_to(edges[facet - 1], (32, 128)), 0.0)
            column = jnp.sum(spill, axis=1, keepdims=True)
            tile = tile + jnp.where(lane == 0, jnp.broadcast_to(column, (32, 128)), 0.0)
        tiles.append(tile)
    group = lane // 32
    moved = [
        [tile if s == 0 else pltpu.roll(tile, 32 * s, 1) for s in range(4)] for tile in tiles
    ]
    rows = []
    for b_lo in range(4):
        halves = []
        for half in range(2):
            value = moved[half * 4][(0 - b_lo) % 4]
            for k in range(1, 4):
                value = jnp.where(group == k, moved[half * 4 + k][(k - b_lo) % 4], value)
            halves.append(value)
        rows.append(jnp.concatenate(halves, axis=1))
    stack = jnp.concatenate(rows, axis=0)
    sign = jnp.where(lax.broadcasted_iota(jnp.int32, (8, 256), 0) < 4, -1.0, 1.0)
    operand = jnp.concatenate([stack, rotate(stack, sign)], axis=1)
    spun = dot(operand, first[...], HI)
    spun = spun * turned_back[0] + rotate(spun, sign) * turned_back[1]
    out = dot(unmix[...], spun, HI)
    upper = lax.broadcasted_iota(jnp.int32, (8, 128), 0) < 4
    block2[...] = jnp.where(upper, out[0:8, 0:128], out[0:8, 128:256])
    relay = links.spread(block2, blocks2, depth_sem2, local_sem2)
    low = lax.broadcasted_iota(jnp.int32, (8, 128), 1) < 64
    sides = jnp.where(low, out[8:16, 0:128], out[16:24, 128:256])
    margin[...] = sides[0:2]
    margin_wait = links.each_depth(lambda d: margin, lambda d: margins.at[z], margin_sem)
    margins[z] = margin[...]
    loop(8, lambda i: keep_second(i + 8))
    relay()
    margin_wait()
    for r in range(16):
        for im in range(2):
            margin_out[im * 16 + r : im * 16 + r + 1, :] = margins[r, im : im + 1, :]
    b_out[...] = blocks2[...]
    links.finish()


def rotate(x, sign):
    groups = x.shape[0] // 8
    out = []
    for g in range(groups):
        out.append(pltpu.roll(x[g * 8 : g * 8 + 8], 4, 0) * sign)
    return jnp.concatenate(out, axis=0)


def weigh(x, dilation, axis):
    n = x.shape[axis]
    near = pltpu.roll(x, dilation, axis) + pltpu.roll(x, n - dilation, axis)
    wide = pltpu.roll(x, 2 * dilation, axis) + pltpu.roll(x, n - 2 * dilation, axis)
    return SPLINE[2] * x + (SPLINE[1] * near + SPLINE[0] * wide)


EXT = COLS + 256
TALL = BAND + 16


def final_kernel(image, one, two, b, margin, phase, waves, thresholds, out):
    v = lax.axis_index("vis")
    f = lax.axis_index("facet")
    edge = jnp.where(v == 0, 0, jnp.where(v == Z * W - 1, 2, 1))
    parts = []
    for im in range(2):
        tiles = [margin[im * 16 : im * 16 + 16, :]]
        for tile in range(16):
            w, l1, mh = tile // 4, (tile // 2) % 2, tile % 2
            tiles.append(b[pl.ds(w * 128 + mh * 4 + im * 2 + l1, 16, stride=8), :])
        tiles.append(margin[im * 16 : im * 16 + 16, :])
        parts.append(jnp.concatenate(tiles, axis=1))
    cos, sin = phase[0:16, 0:1], phase[16:32, 0:1]
    col = lax.broadcasted_iota(jnp.int32, (32, EXT), 1)
    low_col = jnp.where(f == 0, 128, 122)
    high_col = jnp.where(f == F - 1, COLS + 128, COLS + 134)
    inside = (col >= low_col) & (col < high_col)
    back = jnp.concatenate(
        [parts[0] * cos - parts[1] * sin, parts[1] * cos + parts[0] * sin], axis=0
    )
    levels = [jnp.where(inside, back, 0.0)]
    for dilation in (1, 2):
        levels.append(jnp.where(inside, weigh(levels[-1], dilation, 1), 0.0))
    operands = []
    for value in levels:
        hi, lo = split(value[:, 128 : 128 + COLS])
        operands.append(jnp.concatenate([hi, lo, hi], axis=0))
    for tile in range(COLS // 256):
        lanes = slice(tile * 256, tile * 256 + 256)
        c0 = image[:, lanes] - dot(waves[edge, 0], operands[0][:, lanes])
        c1 = one[:, lanes] - dot(waves[edge, 1], operands[1][:, lanes])
        c2 = two[:, lanes] - dot(waves[edge, 2], operands[2][:, lanes])
        d0, d1 = c0 - c1, c1 - c2
        t0, t1 = thresholds[0], thresholds[1]
        kept = (d0 - jnp.clip(d0, -t0, t0)) + (d1 - jnp.clip(d1, -t1, t1))
        out[:, lanes] = jnp.maximum(kept + c2, 0.0)


def vmem(count):
    return [pl.BlockSpec(memory_space=pltpu.VMEM)] * count


def anywhere(count):
    return [pl.BlockSpec(memory_space=pl.ANY)] * count


def sds(*shape, dtype=f32):
    return jax.ShapeDtypeStruct(shape, dtype)


LIMIT = 48 * 1024 * 1024


def pairs(count):
    return pltpu.SemaphoreType.DMA((2, count))


def on_device(
    image, observed, weights, row_cell, col_cell, row_offset, col_offset, kernel, thresholds
):
    root = math.sqrt(NPIX)
    scale = STEP * NPIX / (4.0 * math.sqrt(VDEV * Z * W * F)) / root / root
    V = pltpu.VMEM

    def row_buffers():
        return [V((384, 128), f32), V((128, 128), f32), V((128, 128), f32), V((8, 128), f32),
                V((256, 128), f32), V((8, 128), f32), V((512, 128), f32)]

    b, margin, one, two = pl.pallas_call(
        main_kernel,
        out_shape=[sds(512, 128), sds(32, 128), sds(BAND, COLS), sds(BAND, COLS)],
        in_specs=anywhere(8) + vmem(7),
        out_specs=vmem(4),
        scratch_shapes=[
            V((TALL, EXT), f32), V((TALL, EXT), f32),
            V((32, 256), f32), V((96, 128), f32), V((2, 48, 256), f32), V((512, 128), f32),
            V((512, 256), f32), V((2, 128, 256), f32), V((24, 128), f32),
            V((256, VDEV), bf16), V((16, VDEV), f32), V((16, VDEV), f32),
            V((480, 256), bf16), V((480, 256), bf16), V((480, VDEV), bf16),
            V((480, VDEV), bf16),
            V((512, 128), f32), V((384, 128), f32), V((128, 128), f32), V((128, 128), f32),
            V((8, 128), f32), V((256, 128), f32), V((8, 128), f32), V((512, 128), f32),
            V((1, 128), f32), V((16, 1, 128), f32),
            V((2, 8, 256), f32), V((8, 512), f32), V((8, 512), f32),
            V((512, 128), f32), V((16, 128), f32), V((384, 128), f32), V((3, 16, 128), f32),
            V((128, 128), f32), V((16, 1, 128), f32), V((128, 128), f32),
            V((16, 1, 128), f32), V((8, 128), f32), V((1, 128), f32),
            V((256, 128), f32), V((8, 1, 128), f32), V((8, 128), f32), V((512, 128), f32),
            V((2, 128), f32), V((16, 2, 128), f32),
            pltpu.SemaphoreType.DMA((16,)),
            pairs(48), pairs(16), pairs(32), pairs(16), pairs(48), pairs(16), pairs(8),
            pairs(48), pairs(16), pairs(32), pairs(16), pairs(48), pairs(4), pairs(16),
            pairs(8), pairs(16),
        ],
        compiler_params=pltpu.CompilerParams(
            vmem_limit_bytes=LIMIT, collective_id=0, has_side_effects=True
        ),
    )(
        image, jnp.asarray(band_waves()), jnp.asarray(forward_mix()),
        jnp.asarray(forward_twist()), jnp.asarray(forward_last() / 128.0),
        jnp.asarray(backward_first()), jnp.asarray(backward_twist()),
        jnp.asarray(backward_mix(scale)),
        kernel.T, observed, weights[None], row_cell[None], col_cell[None],
        row_offset[None], col_offset[None],
    )
    v = lax.axis_index("vis")
    phase = lax.dynamic_index_in_dim(jnp.asarray(band_phases()), v, 0, False)
    return pl.pallas_call(
        final_kernel,
        out_shape=sds(BAND, COLS),
        in_specs=vmem(7) + [pl.BlockSpec(memory_space=pltpu.SMEM)],
        out_specs=pl.BlockSpec(memory_space=pltpu.VMEM),
        compiler_params=pltpu.CompilerParams(vmem_limit_bytes=LIMIT),
    )(image, one, two, b, margin, phase, jnp.asarray(gradient_tables()), thresholds)


def solution(mesh):
    return jax.shard_map(
        on_device,
        mesh=mesh,
        in_specs=(
            P("vis", "facet"),
            P(None, ("vis", "facet")),
            P(("vis", "facet")),
            P(("vis", "facet")),
            P(("vis", "facet")),
            P(("vis", "facet")),
            P(("vis", "facet")),
            P(),
            P(),
        ),
        out_specs=P("vis", "facet"),
        check_vma=False,
    )
```

```python
import functools
import math

import jax
import jax.numpy as jnp
import numpy as np
from jax import lax
from jax.experimental import pallas as pl
from jax.experimental.pallas import tpu as pltpu
from jax.sharding import PartitionSpec as P

NPIX = 16384
ROWS = 16
BAND = 256
COLS = 2048
Z = 16
W = 4
F = 8
KW = 8
VDEV = 2048
TAPS = 15
STEP = 0.5
SPLINE = (0.0625, 0.25, 0.375, 0.25, 0.0625)
MESH = pl.DeviceIdType.MESH
HI = lax.Precision.HIGHEST
f32 = jnp.float32
bf16 = jnp.bfloat16


def turn(value, period):
    return 2.0 * np.pi * (np.asarray(value, np.int64) % period).astype(np.float64) / period


def forward_mix():
    f = np.arange(F)[:, None, None]
    l = (2 * np.arange(W)[:, None] + np.arange(2)[None, :])[None]
    f, l = np.broadcast_arrays(f, l)

    def row(j, b, im):
        ang = turn(8 * f * j + 8 * l * b + l * j, 64)
        c, s = np.cos(ang), np.sin(ang)
        pair = (c, s) if im == 0 else (-s, c)
        return np.stack(pair, axis=2).reshape(-1)

    def quarter(j, b, im):
        return row(j, b, 1) if im == 0 else -row(j, b, 0)

    out = np.zeros((W, 96, 128))
    for w in range(W):
        rows = []
        for b_lo in range(4):
            for kind in (row, quarter):
                for im in range(2):
                    for j2 in range(2):
                        for h in range(2):
                            rows.append(kind(2 * w + j2, 4 * h + b_lo, im))
        for kind in (row, quarter):
            for im in range(2):
                for j in range(8):
                    rows.append(kind(j, 0, im))
        out[w] = np.stack(rows)
    return out.astype(np.float32)


def forward_freqs():
    out = np.zeros((W, 48), np.int32)
    for w in range(W):
        rows = [
            8 * (4 * h + b_lo) + 2 * w + j2
            for b_lo in range(4)
            for _ in range(2)
            for j2 in range(2)
            for h in range(2)
        ]
        rows += [2048 + j for _ in range(2) for j in range(8)]
        out[w] = rows
    return out


def forward_last():
    m = np.arange(256)[:, None]
    a = np.tile(np.arange(32), 4)[None, :]
    ang = turn(m * a, 256)
    return (np.concatenate([np.cos(ang), np.sin(ang)], axis=0) / 128.0).astype(np.float32)


def backward_first():
    t = np.arange(256)[:, None]
    m = np.arange(256)[None, :]
    ang = turn(t * m, 256)
    return np.concatenate([np.cos(ang), np.sin(ang)], axis=0).astype(np.float32)


def backward_order():
    return [
        (2 * w + j2, 4 * h + b_lo, im)
        for b_lo in range(4)
        for w in range(W)
        for im in range(2)
        for j2 in range(2)
        for h in range(2)
    ]


def backward_twist():
    freq = np.array([j + 8 * b for j, b, _ in backward_order()])[:, None]
    ang = turn(freq * np.arange(256)[None, :], NPIX)
    return np.stack([np.cos(ang), np.sin(ang)]).astype(np.float32)


def backward_mix(scale):
    order = backward_order()
    j = np.array([o[0] for o in order])
    b = np.array([o[1] for o in order])
    im_in = np.array([o[2] for o in order])

    def row(f, l, im):
        ang = turn(8 * f * j + 8 * l * b + l * j, 64)
        c, s = np.cos(ang), np.sin(ang)
        if im == 0:
            return np.where(im_in == 0, c, -s)
        return np.where(im_in == 0, s, c)

    out = np.zeros((F * W, 24, 128))
    for f in range(F):
        for w in range(W):
            here = out[f * W + w]
            for copy in range(2):
                for im in range(2):
                    for l1 in range(2):
                        here[copy * 4 + im * 2 + l1] = row(f, 2 * w + l1, im)
            for im in range(2):
                here[8 + im] = row(f, 8, im)
                here[16 + im] = row(f, -1, im)
    return (out * scale).astype(np.float32)


def split(x):
    hi = x.astype(bf16)
    return hi, (x - hi.astype(f32)).astype(bf16)


def split_host(x):
    hi = x.astype(jnp.bfloat16)
    lo = (x - hi.astype(np.float64)).astype(jnp.bfloat16)
    return hi, lo


def row_waves():
    u = np.arange(ROWS)[:, None] + NPIX // 8
    ang = turn(u * np.arange(-8, BAND + 8)[None, :], NPIX)
    return np.concatenate([np.cos(ang), -np.sin(ang)], axis=0)


def smooth_rows(x, dilation):
    out = np.zeros_like(x)
    for s, weight in zip(range(-2, 3), SPLINE):
        out += weight * np.roll(x, -s * dilation, axis=1)
    return out


def gradient_tables():
    out = np.zeros((3, 3, BAND, 96), jnp.bfloat16)
    base = row_waves()
    inside = np.ones((3, BAND + 16))
    inside[0, :8] = 0
    inside[2, BAND + 8 :] = 0
    for edge in range(3):
        level = base
        for step in range(3):
            if step:
                level = smooth_rows(level * inside[edge], 2 ** (step - 1))
            hi, lo = split_host(level[:, 8 : 8 + BAND].T)
            out[edge, step] = np.concatenate([hi, hi, lo], axis=1)
    return out


def dot(a, b, precision=None):
    return jnp.dot(a, b, preferred_element_type=f32, precision=precision)


def position():
    v = lax.axis_index("vis")
    return v, v // W, v % W, lax.axis_index("facet")


def band_waves():
    rows = np.arange(Z * W)[:, None] * BAND + np.arange(BAND)[None, :]
    u = NPIX // 8 + np.arange(ROWS)
    ang = turn(u[None, :, None] * rows[:, None, :], NPIX)
    return np.concatenate([np.cos(ang), -np.sin(ang)], axis=1).astype(np.float32)


def forward_twist():
    freq = np.arange(F)[:, None, None] * COLS + forward_freqs()[None]
    ang = turn(freq.reshape(F * W, 48, 1) * np.arange(256), NPIX)
    return np.stack([np.cos(ang), np.sin(ang)], axis=1).astype(np.float32)


def band_phases():
    u = NPIX // 8 + np.arange(ROWS)
    ang = turn(u[None, :] * (np.arange(Z * W)[:, None] * BAND), NPIX)
    both = np.concatenate([np.cos(ang), np.sin(ang)], axis=1)
    return np.broadcast_to(both[:, :, None], (Z * W, 32, 128)).astype(np.float32)


def loop(count, body):
    def step(i, carry):
        body(i)
        return carry

    lax.fori_loop(0, count, step, 0)


def far_first(i):
    k = (i + 1) // 2
    return 8 + k - 2 * k * (i % 2)


FACETS_FAR_FIRST = (3, 5, 1, 7, 4, 2, 6, 0)


def rows8(ref, slot):
    return ref.at[pl.ds(pl.multiple_of(slot * 8, 8), 8)]


class Links:
    def __init__(self):
        self.v, self.z, self.w, self.f = position()
        self.pending = []

    def local(self, d):
        return (self.z * W + (self.w + d) % W, self.f)

    def depth(self, d):
        return (((self.z + d) % Z) * W + self.w, self.f)

    def plane(self, df, dw):
        return (self.z * W + (self.w + dw) % W, (self.f + df) % F)

    def copy(self, src, dst, send, recv, peer):
        return pltpu.make_async_remote_copy(
            src_ref=src, dst_ref=dst, send_sem=send, recv_sem=recv,
            device_id=peer, device_id_type=MESH,
        )

    def bytes_of(self, ref, sem):
        return self.copy(ref, ref, sem, sem, self.depth(1))

    def greet(self, extra):
        barrier = pltpu.get_barrier_semaphore()

        def signal(peer):
            pl.semaphore_signal(barrier, inc=1, device_id=peer, device_id_type=MESH)

        loop(Z - 1, lambda i: signal(self.depth(far_first(i))))
        for df in FACETS_FAR_FIRST:
            first = 0 if df else 1
            loop(W - first, lambda i: signal(self.plane(df, i + first)))
        for peer in extra:
            signal(peer)
        count = (Z - 1) + (F * W - 1) + len(extra)
        return lambda: pl.semaphore_wait(barrier, count)

    def later(self, wait):
        self.pending.append(wait)

    def finish(self):
        for wait in self.pending:
            wait()

    def reduce_rows(self, parts, near, near_sem, summed, far, far_sem):
        def send_row(row):
            for d in range(1, W):
                here = ((self.w + d) % W) * Z + row
                self.copy(
                    rows8(parts, here), rows8(near, row * (W - 1) + d - 1), near_sem.at[Z],
                    near_sem.at[row], self.local(d),
                ).start()

        def sum_row(row):
            start = pl.multiple_of(row * (8 * (W - 1)), 8)
            self.bytes_of(near.at[pl.ds(start, 8 * (W - 1))], near_sem.at[row]).wait_recv()
            value = parts[pl.ds(pl.multiple_of((self.w * Z + row) * 8, 8), 8), :]
            for d in range(W - 1):
                value = value + near[pl.ds(pl.multiple_of(start + d * 8, 8), 8), :]
            summed[pl.ds(pl.multiple_of(row * 8, 8), 8), :] = value

        loop(Z - 1, lambda i: send_row((self.z + far_first(i)) % Z))
        send_row(self.z)

        def forward():
            def step(i):
                d = far_first(i)
                row = (self.z + d) % Z
                sum_row(row)
                self.copy(
                    rows8(summed, row), rows8(far, d - 1), far_sem.at[0], far_sem.at[1],
                    self.depth(d),
                ).start()

            loop(Z - 1, step)
            sum_row(self.z)

        def result():
            self.bytes_of(far, far_sem.at[1]).wait_recv()
            value = summed[pl.ds(pl.multiple_of(self.z * 8, 8), 8), :]
            for d in range(Z - 1):
                value = value + far[d * 8 : d * 8 + 8]
            return value

        self.later(self.bytes_of(near, near_sem.at[Z]).wait_send)
        self.later(self.bytes_of(far, far_sem.at[0]).wait_send)
        return forward, result

    def share_plane(self, mine, gathered, sem):
        own = self.f * W + self.w
        for df in FACETS_FAR_FIRST:
            first = 0 if df else 1
            loop(
                W - first,
                lambda i: self.copy(
                    mine, rows8(gathered, own), sem.at[0], sem.at[1],
                    self.plane(df, i + first),
                ).start(),
            )
        gathered[pl.ds(pl.multiple_of(own * 8, 8), 8), :] = mine[...]
        whole = gathered.at[pl.ds(0, 8 * (F * W - 1))]
        self.later(self.bytes_of(whole, sem.at[0]).wait_send)
        return self.bytes_of(whole, sem.at[1]).wait_recv

    def spread(self, block, blocks, depth_sem, local_sem):
        def depth_copy(d):
            return self.copy(
                block, rows8(blocks, self.w * Z + self.z), depth_sem.at[0], depth_sem.at[d],
                self.depth(d),
            )

        def pass_on(row):
            slot = rows8(blocks, self.w * Z + row)
            for d in range(1, W):
                self.copy(
                    slot, slot, local_sem.at[0], local_sem.at[1], self.local(d)
                ).start()

        loop(Z - 1, lambda i: depth_copy(far_first(i)).start())
        blocks[pl.ds(pl.multiple_of((self.w * Z + self.z) * 8, 8), 8), :] = block[...]
        pass_on(self.z)
        others = blocks.at[pl.ds(0, 128 * (W - 1))]

        def relay():
            def step(i):
                d = far_first(Z - 2 - i)
                depth_copy(d).wait_recv()
                pass_on((self.z - d + Z) % Z)

            loop(Z - 1, step)
            self.bytes_of(others, local_sem.at[1]).wait_recv()

        self.later(self.bytes_of(blocks.at[pl.ds(0, 8 * (Z - 1))], depth_sem.at[0]).wait_send)
        self.later(self.bytes_of(others, local_sem.at[0]).wait_send)
        return relay

    def each_depth(self, src, dst, held, sem):
        def send(i):
            d = far_first(i)
            self.copy(src(d), dst(d), sem.at[0], sem.at[1], self.depth(d)).start()

        loop(Z - 1, send)
        whole = held.at[pl.ds(0, Z - 1)]
        self.later(self.bytes_of(whole, sem.at[0]).wait_send)
        return self.bytes_of(whole, sem.at[1]).wait_recv


EXT = COLS + 256
TALL = BAND + 16
CHUNKS = 4


def main_kernel(
    image, waves_all, mix_all, twist_all, last_hbm, first_hbm, turn_hbm, unmix_all,
    phase_all, slopes_hbm, kernel_hbm, observed_hbm, weights_hbm, row_cell_hbm, col_cell_hbm, row_offset_hbm,
    col_offset_hbm,
    thresholds, out_hbm,
    kernel_t, observed, weights, row_cell, col_cell, row_offset, col_offset,
    phase, slopes, out, one, two, ext, across, waves, mix, twist, last, first, turned_back, unmix,
    pick, col_taps_all, row_taps_all, table_hi, table_lo, values_hi, values_lo,
    parts, near, summed, far, mine, gathered, block, blocks, rim_row, rims,
    pack, left, right,
    g, edge, near2, near_edge, summed2, summed_edge, far2, far_edge, mine2, mine_edge,
    gathered2, edges, block2, blocks2, margin, margins,
    load_sem, near_sem, far_sem, plane_sem, depth_sem, local_sem, rim_sem, halo_sem,
    near_sem2, far_sem2, plane_sem2, depth_sem2, local_sem2, near_edge_sem, far_edge_sem,
    edge_sem, margin_sem, store_sem,
):
    links = Links()
    v, z, w, f = links.v, links.z, links.w, links.f
    own = f * W + w
    vs = ((v + Z * W - 1) % (Z * W), v, (v + 1) % (Z * W))
    fs = ((f + F - 1) % F, f, (f + 1) % F)
    ring = [(vs[i], fs[k]) for i in range(3) for k in range(3) if (i, k) != (1, 1)]
    gathered_in = links.greet(ring)

    loads = []

    def load(src, dst):
        loads.append(pltpu.make_async_copy(src, dst, load_sem.at[len(loads)]))
        loads[-1].start()
        return loads[-1]

    span = COLS // CHUNKS
    early_loads = [
        load(kernel_hbm, kernel_t), load(row_cell_hbm, row_cell), load(col_cell_hbm, col_cell),
        load(row_offset_hbm, row_offset), load(col_offset_hbm, col_offset),
    ]
    wave_load = load(waves_all.at[v], waves)
    chunk_loads = [
        load(
            image.at[:, pl.ds(c * span, span)],
            ext.at[pl.ds(8, BAND), pl.ds(128 + c * span, span)],
        )
        for c in range(CHUNKS)
    ]
    forward_loads = [
        load(observed_hbm, observed), load(weights_hbm, weights),
        load(mix_all.at[w], mix), load(twist_all.at[own], twist), load(last_hbm, last),
    ]
    backward_loads = [
        load(phase_all.at[v], phase), load(slopes_hbm, slopes),
        load(first_hbm, first), load(turn_hbm, turned_back), load(unmix_all.at[own], unmix),
    ]

    for copy in early_loads:
        copy.wait()
    o_of = lax.broadcasted_iota(jnp.int32, (16, 256), 1) // 16
    s_of = lax.broadcasted_iota(jnp.int32, (16, 256), 1) % 16
    rep = (lax.broadcasted_iota(jnp.int32, (16, 256), 0) == o_of).astype(f32)
    fanned = dot(kernel_t[...], rep, HI)
    padded = jnp.concatenate([fanned, jnp.zeros((8, 256), f32)], axis=0)
    tap_table = jnp.where(s_of == 0, padded, 0.0)
    for s in range(1, 9):
        tap_table = jnp.where(s_of == s, pltpu.roll(padded, s, 0), tap_table)
    tap_hi, tap_lo = split(tap_table)
    tap_both = jnp.concatenate([tap_hi, tap_lo], axis=0)
    down = lax.broadcasted_iota(jnp.int32, (256, 256), 0)
    first_col = f * COLS

    def onehot(index):
        return jnp.where(down == index, 1.0, 0.0).astype(bf16)

    def choose(step):
        lanes = pl.ds(pl.multiple_of(step * 256, 256), 256)
        col = col_cell[:, lanes] - first_col
        q = col // 8
        pick[:, lanes] = onehot((q % 8) * 32 + q // 8)
        col_taps = dot(tap_both, onehot(col_offset[:, lanes] * 16 + col % 8))
        col_taps_all[:, lanes] = col_taps[:16] + col_taps[16:]
        row_taps = dot(tap_both, onehot(row_offset[:, lanes] * 16 + row_cell[:, lanes]))
        row_taps_all[:, lanes] = row_taps[:16] + row_taps[16:]

    wave_load.wait()
    wave_hi, wave_lo = split(waves[...])
    both = jnp.concatenate([wave_hi, wave_lo], axis=0)
    for tile in range(8):
        if tile % (8 // CHUNKS) == 0:
            chunk_loads[tile // (8 // CHUNKS)].wait()
        hi, lo = split(ext[8 : 8 + BAND, 128 + tile * 256 : 384 + tile * 256])
        value = dot(both, hi)
        value = value[:32] + value[32:] + dot(wave_hi, lo)
        for half in range(2):
            c = (tile % 2) * 2 + half
            for im in range(2):
                parts[pl.ds((tile // 2) * 128 + im * 4 + c, 16, stride=8), :] = value[
                    im * 16 : im * 16 + 16, half * 128 : half * 128 + 128
                ]
    pack[0] = jnp.transpose(ext[8 : 8 + BAND, 128:256])[0:8]
    pack[1] = jnp.transpose(ext[8 : 8 + BAND, COLS : COLS + 128])[120:128]
    gathered_in()
    forward, result = links.reduce_rows(parts, near, near_sem, summed, far, far_sem)
    halo = []

    def halo_copy(src, dst, peer):
        halo.append(
            links.copy(src, dst, halo_sem.at[0, len(halo)], halo_sem.at[1, len(halo)], peer)
        )
        halo[-1].start()

    middle = pl.ds(128, COLS)
    halo_copy(ext.at[pl.ds(8, 8), middle], ext.at[pl.ds(BAND + 8, 8), middle], (vs[0], fs[1]))
    halo_copy(ext.at[pl.ds(BAND, 8), middle], ext.at[pl.ds(0, 8), middle], (vs[2], fs[1]))
    halo_copy(pack.at[0], right.at[:, pl.ds(128, 256)], (vs[1], fs[0]))
    halo_copy(pack.at[1], left.at[:, pl.ds(128, 256)], (vs[1], fs[2]))
    halo_copy(pack.at[0, :, pl.ds(0, 128)], right.at[:, pl.ds(384, 128)], (vs[0], fs[0]))
    halo_copy(pack.at[0, :, pl.ds(128, 128)], right.at[:, pl.ds(0, 128)], (vs[2], fs[0]))
    halo_copy(pack.at[1, :, pl.ds(0, 128)], left.at[:, pl.ds(384, 128)], (vs[0], fs[2]))
    halo_copy(pack.at[1, :, pl.ds(128, 128)], left.at[:, pl.ds(0, 128)], (vs[2], fs[2]))
    forward()

    low_row = jnp.where(v == 0, 8, 0)
    high_row = jnp.where(v == Z * W - 1, BAND + 8, TALL)
    low_col = jnp.where(f == 0, 128, 0)
    high_col = jnp.where(f == F - 1, COLS + 128, EXT)
    tall = lax.broadcasted_iota(jnp.int32, (TALL, 128), 0)
    rows_in = (tall >= low_row) & (tall < high_row)

    def assemble():
        for copy in halo:
            copy.wait()
        ext[0:8, middle] = jnp.where(low_row == 0, ext[0:8, middle], 0.0)
        bottom = pl.ds(BAND + 8, 8)
        ext[bottom, middle] = jnp.where(high_row == TALL, ext[bottom, middle], 0.0)
        side = jnp.concatenate([jnp.zeros((120, 512), f32), left[...]], axis=0)
        side = jnp.transpose(side)[120 : 120 + TALL]
        ext[:, 0:128] = jnp.where(rows_in & (low_col == 0), side, 0.0)
        side = jnp.concatenate([right[...], jnp.zeros((120, 512), f32)], axis=0)
        side = jnp.transpose(side)[120 : 120 + TALL]
        ext[:, EXT - 128 : EXT] = jnp.where(rows_in & (high_col == EXT), side, 0.0)

    def along_columns(ext, dilation):
        def step(i):
            rows = pl.ds(pl.multiple_of(i * 8, 8), 8)
            across[rows, :] = weigh(ext[rows, :], dilation, 1)

        loop(TALL // 8, step)

    def smoothed_rows(i, dilation):
        lanes = pl.ds(pl.multiple_of(i * 128, 128), 128)
        return lanes, weigh(across[:, lanes], dilation, 0)

    def first_rows(i):
        lanes, value = smoothed_rows(i, 1)
        col = lax.broadcasted_iota(jnp.int32, (TALL, 128), 1) + i * 128
        value = jnp.where(rows_in & (col >= low_col) & (col < high_col), value, 0.0)
        one[:, lanes] = value

    def keep_second(i):
        lanes, value = smoothed_rows(i + 1, 2)
        two[:, pl.ds(pl.multiple_of(i * 128, 128), 128)] = value[8 : 8 + BAND]

    assemble()
    along_columns(ext, 1)
    total = result()
    mine[...] = total
    plane_wait = links.share_plane(mine, gathered, plane_sem)
    loop(VDEV // 256, choose)
    for copy in forward_loads:
        copy.wait()
    plane_wait()

    wide = jnp.concatenate(
        [gathered[pl.ds(0, 128, stride=2), :], gathered[pl.ds(1, 128, stride=2), :]], axis=1
    )
    mixed = dot(mix[...], wide, HI)
    cos, sin = twist[0], twist[1]
    turned_a, turned_b = [], []
    for part in range(5):
        size = 16 if part == 4 else 8
        a = mixed[part * 16 : part * 16 + size]
        b = mixed[part * 16 + size : part * 16 + 2 * size]
        c = cos[part * 8 : part * 8 + size]
        s = sin[part * 8 : part * 8 + size]
        turned_a.append(a * c + b * s)
        turned_b.append(b * c - a * s)
    turned = jnp.concatenate(
        [jnp.concatenate(turned_a, axis=0), jnp.concatenate(turned_b, axis=0)], axis=1
    )
    spec = dot(turned, last[...], HI)
    group8 = lax.broadcasted_iota(jnp.int32, (8, 128), 1) // 32
    value = spec[0:8]
    for b_lo in range(1, 4):
        value = jnp.where(group8 == b_lo, spec[b_lo * 8 : b_lo * 8 + 8], value)
    block[...] = value
    relay = links.spread(block, blocks, depth_sem, local_sem)
    diagonal = lax.broadcasted_iota(jnp.int32, (16, 128), 0) == lax.broadcasted_iota(
        jnp.int32, (16, 128), 1
    )
    corner = jnp.where(diagonal, jnp.broadcast_to(spec[32:48, 0:1], (16, 128)), 0.0)
    rim_row[...] = jnp.sum(corner, axis=0, keepdims=True)
    rim_wait = links.each_depth(lambda d: rim_row, lambda d: rims.at[z], rims, rim_sem)
    rims[z] = rim_row[...]
    loop(EXT // 128, first_rows)
    relay()
    rim_wait()

    lane = lax.broadcasted_iota(jnp.int32, (32, 256), 1)
    rim = jnp.concatenate([rims[r] for r in range(16)], axis=0)
    for j in range(8):
        both = []
        for im in range(2):
            halves = [
                blocks[pl.ds((j // 2) * 128 + im * 4 + (j % 2) * 2 + h, 16, stride=8), :]
                for h in range(2)
            ]
            both.append(jnp.concatenate(halves, axis=1))
        tile = jnp.concatenate(both, axis=0)
        hi, lo = split(tile)
        table_hi[j * 32 : j * 32 + 32, :] = hi
        table_lo[j * 32 : j * 32 + 32, :] = lo
        if j < 7:
            beyond = jnp.concatenate(
                [
                    jnp.broadcast_to(rim[:, im * 8 + j : im * 8 + j + 1], (16, 256))
                    for im in range(2)
                ],
                axis=0,
            )
            once = pltpu.roll(tile, 224, 1)
            twice = pltpu.roll(once, 255, 1)
            moved = jnp.where(lane < 224, once, jnp.where(lane == 255, beyond, twice))
            hi, lo = split(moved)
            table_hi[(j + 8) * 32 : (j + 9) * 32, :] = hi
            table_lo[(j + 8) * 32 : (j + 9) * 32, :] = lo

    def visit(step):
        lanes = pl.ds(pl.multiple_of(step * 256, 256), 256)
        chosen = pick[:, lanes]
        col_taps = col_taps_all[:, lanes]
        row_taps = row_taps_all[:, lanes]
        picked = dot(table_hi[...], chosen) + dot(table_lo[...], chosen)
        folded = picked[0:32] * col_taps[0:1]
        for d in range(1, TAPS):
            folded = folded + picked[d * 32 : d * 32 + 32] * col_taps[d : d + 1]
        misfit = []
        for im in range(2):
            model = jnp.sum(folded[im * 16 : im * 16 + 16] * row_taps, axis=0, keepdims=True)
            misfit.append(
                row_taps * (weights[:, lanes] * (model - observed[im : im + 1, lanes]))
            )
        fan = jnp.concatenate(misfit, axis=0)
        for d in range(TAPS):
            hi, lo = split(fan * col_taps[d : d + 1])
            values_hi[d * 32 : d * 32 + 32, lanes] = hi
            values_lo[d * 32 : d * 32 + 32, lanes] = lo

    loop(VDEV // 256, visit)

    def scatter(values):
        return lax.dot_general(
            values[...], pick[...], (((1,), (1,)), ((), ())), preferred_element_type=f32
        )

    grid = scatter(values_hi) + scatter(values_lo)
    lane_half = lax.broadcasted_iota(jnp.int32, (16, 128), 1)
    over_edge = [jnp.zeros((16, 128), f32)]
    for j in range(8):
        tile = grid[j * 32 : j * 32 + 32]
        if j < 7:
            over = grid[(j + 8) * 32 : (j + 9) * 32]
            once = pltpu.roll(over, 32, 1)
            twice = pltpu.roll(once, 1, 1)
            tile = tile + jnp.where(lane >= 32, once, jnp.where(lane == 0, 0.0, twice))
            for im in range(2):
                end = over[im * 16 : im * 16 + 16, 255:256]
                over_edge.append(
                    jnp.where(lane_half == im * 8 + j, jnp.broadcast_to(end, (16, 128)), 0.0)
                )
        for im in range(2):
            for h in range(2):
                g[pl.ds((j // 2) * 128 + im * 4 + (j % 2) * 2 + h, 16, stride=8), :] = tile[
                    im * 16 : im * 16 + 16, h * 128 : h * 128 + 128
                ]
    edge[...] = functools.reduce(jnp.add, over_edge)

    forward, result = links.reduce_rows(g, near2, near_sem2, summed2, far2, far_sem2)
    for d in range(1, W):
        links.copy(
            edge, near_edge.at[d - 1], near_edge_sem.at[0], near_edge_sem.at[1], links.local(d)
        ).start()
    links.later(links.bytes_of(near_edge, near_edge_sem.at[0]).wait_send)
    forward()
    links.bytes_of(near_edge, near_edge_sem.at[1]).wait_recv()
    edge_sum = edge[...] + near_edge[0] + near_edge[1] + near_edge[2]
    for r in range(16):
        summed_edge[r] = edge_sum[r : r + 1]
    edge_wait = links.each_depth(
        lambda d: summed_edge.at[(z + d) % Z], lambda d: far_edge.at[d - 1], far_edge,
        far_edge_sem,
    )
    along_columns(one, 2)
    total = result()
    mine2[...] = total
    plane_wait = links.share_plane(mine2, gathered2, plane_sem2)
    edge_wait()
    edge_total = summed_edge[z]
    for d in range(Z - 1):
        edge_total = edge_total + far_edge[d]
    mine_edge[...] = edge_total
    for df in FACETS_FAR_FIRST[:-1]:
        links.copy(
            mine_edge, edges.at[f], edge_sem.at[0], edge_sem.at[1], links.plane(df, 0)
        ).start()
    links.later(links.bytes_of(edges.at[pl.ds(0, F - 1)], edge_sem.at[0]).wait_send)
    edges[f] = edge_total
    loop(8, keep_second)
    for copy in backward_loads:
        copy.wait()
    links.bytes_of(edges.at[pl.ds(0, F - 1)], edge_sem.at[1]).wait_recv()
    plane_wait()

    row_index = lax.broadcasted_iota(jnp.int32, (32, 128), 0)
    lane = lax.broadcasted_iota(jnp.int32, (32, 128), 1)
    target = ((row_index // 4) % 2) * 8 + 2 * (row_index // 8) + (row_index // 2) % 2
    wanted = (lane == target) & (row_index % 2 == 0)
    tiles = []
    for facet in range(F):
        tile = gathered2[facet * 32 : facet * 32 + 32]
        if facet:
            spill = jnp.where(wanted, jnp.broadcast_to(edges[facet - 1], (32, 128)), 0.0)
            column = jnp.sum(spill, axis=1, keepdims=True)
            tile = tile + jnp.where(lane == 0, jnp.broadcast_to(column, (32, 128)), 0.0)
        tiles.append(tile)
    group = lane // 32
    moved = [
        [tile if s == 0 else pltpu.roll(tile, 32 * s, 1) for s in range(4)] for tile in tiles
    ]
    rows = []
    for b_lo in range(4):
        halves = []
        for half in range(2):
            value = moved[half * 4][(0 - b_lo) % 4]
            for k in range(1, 4):
                value = jnp.where(group == k, moved[half * 4 + k][(k - b_lo) % 4], value)
            halves.append(value)
        rows.append(jnp.concatenate(halves, axis=1))
    stack = jnp.concatenate(rows, axis=0)
    sign = jnp.where(lax.broadcasted_iota(jnp.int32, (8, 256), 0) < 4, -1.0, 1.0)
    operand = jnp.concatenate([stack, rotate(stack, sign)], axis=1)
    spun = dot(operand, first[...], HI)
    spun = spun * turned_back[0] + rotate(spun, sign) * turned_back[1]
    solved = dot(unmix[...], spun, HI)
    upper = lax.broadcasted_iota(jnp.int32, (8, 128), 0) < 4
    block2[...] = jnp.where(upper, solved[0:8, 0:128], solved[0:8, 128:256])
    relay = links.spread(block2, blocks2, depth_sem2, local_sem2)
    low = lax.broadcasted_iota(jnp.int32, (8, 128), 1) < 64
    sides = jnp.where(low, solved[8:16, 0:128], solved[16:24, 128:256])
    margin[...] = sides[0:2]
    margin_wait = links.each_depth(lambda d: margin, lambda d: margins.at[z], margins, margin_sem)
    margins[z] = margin[...]
    loop(8, lambda i: keep_second(i + 8))
    relay()
    margin_wait()

    variant = (v + Z * W - 1) // (Z * W) + (v + 1) // (Z * W)
    parts = []
    for im in range(2):
        rim = jnp.concatenate([margins[r, im : im + 1, :] for r in range(16)], axis=0)
        tiles = [rim]
        for tile in range(16):
            start = (tile // 4) * 128 + (tile % 2) * 4 + im * 2 + (tile // 2) % 2
            tiles.append(blocks2[pl.ds(start, 16, stride=8), :])
        tiles.append(rim)
        parts.append(jnp.concatenate(tiles, axis=1))
    cos, sin = phase[0:16, 0:1], phase[16:32, 0:1]
    col = lax.broadcasted_iota(jnp.int32, (32, EXT), 1)
    inside = (col >= jnp.where(f == 0, 128, 122)) & (
        col < jnp.where(f == F - 1, COLS + 128, COLS + 134)
    )
    back = jnp.concatenate(
        [parts[0] * cos - parts[1] * sin, parts[1] * cos + parts[0] * sin], axis=0
    )
    levels = [jnp.where(inside, back, 0.0)]
    for dilation in (1, 2):
        levels.append(jnp.where(inside, weigh(levels[-1], dilation, 1), 0.0))
    operands = []
    for value in levels:
        hi, lo = split(value[:, 128 : 128 + COLS])
        operands.append(jnp.concatenate([hi, lo, hi], axis=0))
    t0, t1 = thresholds[0], thresholds[1]
    stores = []
    for tile in range(COLS // 256):
        lanes = slice(tile * 256, tile * 256 + 256)
        held = slice(128 + tile * 256, 384 + tile * 256)
        c0 = ext[8 : 8 + BAND, held] - dot(slopes[variant, 0], operands[0][:, lanes])
        c1 = one[8 : 8 + BAND, held] - dot(slopes[variant, 1], operands[1][:, lanes])
        c2 = two[:, lanes] - dot(slopes[variant, 2], operands[2][:, lanes])
        d0, d1 = c0 - c1, c1 - c2
        kept = (d0 - jnp.clip(d0, -t0, t0)) + (d1 - jnp.clip(d1, -t1, t1))
        out[:, lanes] = kept + c2
        region = pl.ds(tile * 256, 256)
        stores.append(
            pltpu.make_async_copy(out.at[:, region], out_hbm.at[:, region], store_sem.at[tile])
        )
        stores[-1].start()
    links.finish()
    for copy in stores:
        copy.wait()


def rotate(x, sign):
    groups = x.shape[0] // 8
    out = []
    for g in range(groups):
        out.append(pltpu.roll(x[g * 8 : g * 8 + 8], 4, 0) * sign)
    return jnp.concatenate(out, axis=0)


def weigh(x, dilation, axis):
    n = x.shape[axis]
    near = pltpu.roll(x, dilation, axis) + pltpu.roll(x, n - dilation, axis)
    wide = pltpu.roll(x, 2 * dilation, axis) + pltpu.roll(x, n - 2 * dilation, axis)
    return SPLINE[2] * x + (SPLINE[1] * near + SPLINE[0] * wide)


EXT = COLS + 256
TALL = BAND + 16


def anywhere(count):
    return [pl.BlockSpec(memory_space=pltpu.HBM)] * count


def sds(*shape, dtype=f32):
    return jax.ShapeDtypeStruct(shape, dtype)


LIMIT = 60 * 1024 * 1024


def pairs(count):
    return pltpu.SemaphoreType.DMA((2, count))


def sems(count):
    return pltpu.SemaphoreType.DMA((count,))


def on_device(
    image, observed, weights, row_cell, col_cell, row_offset, col_offset, kernel, thresholds
):
    root = math.sqrt(NPIX)
    scale = STEP * NPIX / (4.0 * math.sqrt(VDEV * Z * W * F)) / root / root
    V = pltpu.VMEM

    result = pl.pallas_call(
        main_kernel,
        out_shape=sds(BAND, COLS),
        in_specs=anywhere(17) + [pl.BlockSpec(memory_space=pltpu.SMEM)],
        out_specs=pl.BlockSpec(memory_space=pltpu.HBM),
        scratch_shapes=[
            V((KW, ROWS), f32), V((2, VDEV), f32), V((1, VDEV), f32),
            V((1, VDEV), jnp.int32), V((1, VDEV), jnp.int32), V((1, VDEV), jnp.int32),
            V((1, VDEV), jnp.int32),
            V((32, 128), f32), V((3, 3, BAND, 96), bf16), V((BAND, COLS), f32),
            V((TALL, EXT), f32), V((BAND, COLS), f32), V((TALL, EXT), f32), V((TALL, EXT), f32),
            V((32, 256), f32), V((96, 128), f32), V((2, 48, 256), f32), V((512, 128), f32),
            V((512, 256), f32), V((2, 128, 256), f32), V((24, 128), f32),
            V((256, VDEV), bf16), V((16, VDEV), f32), V((16, VDEV), f32),
            V((480, 256), bf16), V((480, 256), bf16), V((480, VDEV), bf16),
            V((480, VDEV), bf16),
            V((512, 128), f32), V((384, 128), f32), V((128, 128), f32), V((120, 128), f32),
            V((8, 128), f32), V((256, 128), f32), V((8, 128), f32), V((512, 128), f32),
            V((1, 128), f32), V((16, 1, 128), f32),
            V((2, 8, 256), f32), V((8, 512), f32), V((8, 512), f32),
            V((512, 128), f32), V((16, 128), f32), V((384, 128), f32), V((3, 16, 128), f32),
            V((128, 128), f32), V((16, 1, 128), f32), V((120, 128), f32),
            V((15, 1, 128), f32), V((8, 128), f32), V((1, 128), f32),
            V((256, 128), f32), V((8, 1, 128), f32), V((8, 128), f32), V((512, 128), f32),
            V((2, 128), f32), V((16, 2, 128), f32),
            pltpu.SemaphoreType.DMA((24,)),
            sems(17), sems(2), sems(2), sems(16), sems(2), sems(2), pairs(8),
            sems(17), sems(2), sems(2), sems(16), sems(2), sems(2), sems(2), sems(2), sems(2),
            sems(8),
        ],
        compiler_params=pltpu.CompilerParams(
            vmem_limit_bytes=LIMIT, collective_id=0, has_side_effects=True
        ),
    )(
        image, jnp.asarray(band_waves()), jnp.asarray(forward_mix()),
        jnp.asarray(forward_twist()), jnp.asarray(forward_last() / 128.0),
        jnp.asarray(backward_first()), jnp.asarray(backward_twist()),
        jnp.asarray(backward_mix(scale)), jnp.asarray(band_phases()),
        jnp.asarray(gradient_tables()), kernel.T, observed, weights[None], row_cell[None],
        col_cell[None], row_offset[None], col_offset[None], thresholds,
    )
    return jnp.maximum(result, 0.0)


def solution(mesh):
    return jax.shard_map(
        on_device,
        mesh=mesh,
        in_specs=(
            P("vis", "facet"),
            P(None, ("vis", "facet")),
            P(("vis", "facet")),
            P(("vis", "facet")),
            P(("vis", "facet")),
            P(("vis", "facet")),
            P(("vis", "facet")),
            P(),
            P(),
        ),
        out_specs=P("vis", "facet"),
        check_vma=False,
    )
```

```python
import functools
import math

import jax
import jax.numpy as jnp
import numpy as np
from jax import lax
from jax.experimental import pallas as pl
from jax.experimental.pallas import tpu as pltpu
from jax.sharding import PartitionSpec as P

NPIX = 16384
ROWS = 16
BAND = 256
COLS = 2048
Z = 16
W = 4
F = 8
KW = 8
VDEV = 2048
TAPS = 15
STEP = 0.5
SPLINE = (0.0625, 0.25, 0.375, 0.25, 0.0625)
MESH = pl.DeviceIdType.MESH
HI = lax.Precision.HIGHEST
f32 = jnp.float32
bf16 = jnp.bfloat16


def turn(value, period):
    return 2.0 * np.pi * (np.asarray(value, np.int64) % period).astype(np.float64) / period


def forward_mix():
    f = np.arange(F)[:, None, None]
    l = (2 * np.arange(W)[:, None] + np.arange(2)[None, :])[None]
    f, l = np.broadcast_arrays(f, l)

    def row(j, b, im):
        ang = turn(8 * f * j + 8 * l * b + l * j, 64)
        c, s = np.cos(ang), np.sin(ang)
        pair = (c, s) if im == 0 else (-s, c)
        return np.stack(pair, axis=2).reshape(-1)

    def quarter(j, b, im):
        return row(j, b, 1) if im == 0 else -row(j, b, 0)

    out = np.zeros((W, 96, 128))
    for w in range(W):
        rows = []
        for b_lo in range(4):
            for kind in (row, quarter):
                for im in range(2):
                    for j2 in range(2):
                        for h in range(2):
                            rows.append(kind(2 * w + j2, 4 * h + b_lo, im))
        for kind in (row, quarter):
            for im in range(2):
                for j in range(8):
                    rows.append(kind(j, 0, im))
        out[w] = np.stack(rows)
    return out.astype(np.float32)


def forward_freqs():
    out = np.zeros((W, 48), np.int32)
    for w in range(W):
        rows = [
            8 * (4 * h + b_lo) + 2 * w + j2
            for b_lo in range(4)
            for _ in range(2)
            for j2 in range(2)
            for h in range(2)
        ]
        rows += [2048 + j for _ in range(2) for j in range(8)]
        out[w] = rows
    return out


def forward_last():
    m = np.arange(256)[:, None]
    a = np.tile(np.arange(32), 4)[None, :]
    ang = turn(m * a, 256)
    return (np.concatenate([np.cos(ang), np.sin(ang)], axis=0) / 128.0).astype(np.float32)


def backward_first():
    t = np.arange(256)[:, None]
    m = np.arange(256)[None, :]
    ang = turn(t * m, 256)
    return np.concatenate([np.cos(ang), np.sin(ang)], axis=0).astype(np.float32)


def backward_order():
    return [
        (2 * w + j2, 4 * h + b_lo, im)
        for b_lo in range(4)
        for w in range(W)
        for im in range(2)
        for j2 in range(2)
        for h in range(2)
    ]


def backward_twist():
    freq = np.array([j + 8 * b for j, b, _ in backward_order()])[:, None]
    ang = turn(freq * np.arange(256)[None, :], NPIX)
    return np.stack([np.cos(ang), np.sin(ang)]).astype(np.float32)


def backward_mix(scale):
    order = backward_order()
    j = np.array([o[0] for o in order])
    b = np.array([o[1] for o in order])
    im_in = np.array([o[2] for o in order])

    def row(f, l, im):
        ang = turn(8 * f * j + 8 * l * b + l * j, 64)
        c, s = np.cos(ang), np.sin(ang)
        if im == 0:
            return np.where(im_in == 0, c, -s)
        return np.where(im_in == 0, s, c)

    out = np.zeros((F * W, 24, 128))
    for f in range(F):
        for w in range(W):
            here = out[f * W + w]
            for copy in range(2):
                for im in range(2):
                    for l1 in range(2):
                        here[copy * 4 + im * 2 + l1] = row(f, 2 * w + l1, im)
            for im in range(2):
                here[8 + im] = row(f, 8, im)
                here[16 + im] = row(f, -1, im)
    return (out * scale).astype(np.float32)


def split(x):
    hi = x.astype(bf16)
    return hi, (x - hi.astype(f32)).astype(bf16)


def split_host(x):
    hi = x.astype(jnp.bfloat16)
    lo = (x - hi.astype(np.float64)).astype(jnp.bfloat16)
    return hi, lo


def row_waves():
    u = np.arange(ROWS)[:, None] + NPIX // 8
    ang = turn(u * np.arange(-8, BAND + 8)[None, :], NPIX)
    return np.concatenate([np.cos(ang), -np.sin(ang)], axis=0)


def smooth_rows(x, dilation):
    out = np.zeros_like(x)
    for s, weight in zip(range(-2, 3), SPLINE):
        out += weight * np.roll(x, -s * dilation, axis=1)
    return out


def gradient_tables():
    out = np.zeros((3, 3, BAND, 96), jnp.bfloat16)
    base = row_waves()
    inside = np.ones((3, BAND + 16))
    inside[0, :8] = 0
    inside[2, BAND + 8 :] = 0
    for edge in range(3):
        level = base
        for step in range(3):
            if step:
                level = smooth_rows(level * inside[edge], 2 ** (step - 1))
            hi, lo = split_host(level[:, 8 : 8 + BAND].T)
            out[edge, step] = np.concatenate([hi, hi, lo], axis=1)
    return out


def dot(a, b, precision=None):
    return jnp.dot(a, b, preferred_element_type=f32, precision=precision)


def dot3(a, b):
    a_hi, a_lo = split(a)
    b_hi, b_lo = split(b)
    return dot(a_hi, b_hi) + (dot(a_hi, b_lo) + dot(a_lo, b_hi))


def position():
    v = lax.axis_index("vis")
    return v, v // W, v % W, lax.axis_index("facet")


def band_waves():
    rows = np.arange(Z * W)[:, None] * BAND + np.arange(BAND)[None, :]
    u = NPIX // 8 + np.arange(ROWS)
    ang = turn(u[None, :, None] * rows[:, None, :], NPIX)
    return np.concatenate([np.cos(ang), -np.sin(ang)], axis=1).astype(np.float32)


def forward_twist():
    freq = np.arange(F)[:, None, None] * COLS + forward_freqs()[None]
    ang = turn(freq.reshape(F * W, 48, 1) * np.arange(256), NPIX)
    return np.stack([np.cos(ang), np.sin(ang)], axis=1).astype(np.float32)


def band_phases():
    u = NPIX // 8 + np.arange(ROWS)
    ang = turn(u[None, :] * (np.arange(Z * W)[:, None] * BAND), NPIX)
    both = np.concatenate([np.cos(ang), np.sin(ang)], axis=1)
    return np.broadcast_to(both[:, :, None], (Z * W, 32, 128)).astype(np.float32)


def loop(count, body):
    def step(i, carry):
        body(i)
        return carry

    lax.fori_loop(0, count, step, 0)


def far_first(i):
    k = (i + 1) // 2
    return 8 + k - 2 * k * (i % 2)


FACETS_FAR_FIRST = (3, 5, 1, 7, 4, 2, 6, 0)


def rows8(ref, slot):
    return ref.at[pl.ds(pl.multiple_of(slot * 8, 8), 8)]


class Links:
    def __init__(self):
        self.v, self.z, self.w, self.f = position()
        self.pending = []

    def local(self, d):
        return (self.z * W + (self.w + d) % W, self.f)

    def depth(self, d):
        return (((self.z + d) % Z) * W + self.w, self.f)

    def plane(self, df, dw):
        return (self.z * W + (self.w + dw) % W, (self.f + df) % F)

    def copy(self, src, dst, send, recv, peer):
        return pltpu.make_async_remote_copy(
            src_ref=src, dst_ref=dst, send_sem=send, recv_sem=recv,
            device_id=peer, device_id_type=MESH,
        )

    def bytes_of(self, ref, sem):
        return self.copy(ref, ref, sem, sem, self.depth(1))

    def greet(self, extra):
        barrier = pltpu.get_barrier_semaphore()

        def signal(peer):
            pl.semaphore_signal(barrier, inc=1, device_id=peer, device_id_type=MESH)

        loop(Z - 1, lambda i: signal(self.depth(far_first(i))))
        for df in FACETS_FAR_FIRST:
            first = 0 if df else 1
            loop(W - first, lambda i: signal(self.plane(df, i + first)))
        for peer in extra:
            signal(peer)
        count = (Z - 1) + (F * W - 1) + len(extra)
        return lambda: pl.semaphore_wait(barrier, count)

    def later(self, wait):
        self.pending.append(wait)

    def finish(self):
        for wait in self.pending:
            wait()

    def reduce_rows(self, parts, near, near_sem, summed, far, far_sem):
        def send_row(row):
            for d in range(1, W):
                here = ((self.w + d) % W) * Z + row
                self.copy(
                    rows8(parts, here), rows8(near, row * (W - 1) + d - 1), near_sem.at[Z],
                    near_sem.at[row], self.local(d),
                ).start()

        def sum_row(row):
            start = pl.multiple_of(row * (8 * (W - 1)), 8)
            self.bytes_of(near.at[pl.ds(start, 8 * (W - 1))], near_sem.at[row]).wait_recv()
            value = parts[pl.ds(pl.multiple_of((self.w * Z + row) * 8, 8), 8), :]
            for d in range(W - 1):
                value = value + near[pl.ds(pl.multiple_of(start + d * 8, 8), 8), :]
            summed[pl.ds(pl.multiple_of(row * 8, 8), 8), :] = value

        loop(Z - 1, lambda i: send_row((self.z + far_first(i)) % Z))
        send_row(self.z)

        def forward():
            def step(i):
                d = far_first(i)
                row = (self.z + d) % Z
                sum_row(row)
                self.copy(
                    rows8(summed, row), rows8(far, d - 1), far_sem.at[0], far_sem.at[1],
                    self.depth(d),
                ).start()

            loop(Z - 1, step)
            sum_row(self.z)

        def result():
            self.bytes_of(far, far_sem.at[1]).wait_recv()
            value = summed[pl.ds(pl.multiple_of(self.z * 8, 8), 8), :]
            for d in range(Z - 1):
                value = value + far[d * 8 : d * 8 + 8]
            return value

        self.later(self.bytes_of(near, near_sem.at[Z]).wait_send)
        self.later(self.bytes_of(far, far_sem.at[0]).wait_send)
        return forward, result

    def share_plane(self, mine, gathered, sem):
        own = self.f * W + self.w
        for df in FACETS_FAR_FIRST:
            first = 0 if df else 1
            loop(
                W - first,
                lambda i: self.copy(
                    mine, rows8(gathered, own), sem.at[0], sem.at[1],
                    self.plane(df, i + first),
                ).start(),
            )
        gathered[pl.ds(pl.multiple_of(own * 8, 8), 8), :] = mine[...]
        whole = gathered.at[pl.ds(0, 8 * (F * W - 1))]
        self.later(self.bytes_of(whole, sem.at[0]).wait_send)
        return self.bytes_of(whole, sem.at[1]).wait_recv

    def spread(self, block, blocks, depth_sem, local_sem):
        def depth_copy(d):
            return self.copy(
                block, rows8(blocks, self.w * Z + self.z), depth_sem.at[0], depth_sem.at[d],
                self.depth(d),
            )

        def pass_on(row):
            slot = rows8(blocks, self.w * Z + row)
            for d in range(1, W):
                self.copy(
                    slot, slot, local_sem.at[0], local_sem.at[1], self.local(d)
                ).start()

        loop(Z - 1, lambda i: depth_copy(far_first(i)).start())
        blocks[pl.ds(pl.multiple_of((self.w * Z + self.z) * 8, 8), 8), :] = block[...]
        pass_on(self.z)
        others = blocks.at[pl.ds(0, 128 * (W - 1))]

        def relay():
            def step(i):
                d = far_first(Z - 2 - i)
                depth_copy(d).wait_recv()
                pass_on((self.z - d + Z) % Z)

            loop(Z - 1, step)
            self.bytes_of(others, local_sem.at[1]).wait_recv()

        self.later(self.bytes_of(blocks.at[pl.ds(0, 8 * (Z - 1))], depth_sem.at[0]).wait_send)
        self.later(self.bytes_of(others, local_sem.at[0]).wait_send)
        return relay

    def each_depth(self, src, dst, held, sem):
        def send(i):
            d = far_first(i)
            self.copy(src(d), dst(d), sem.at[0], sem.at[1], self.depth(d)).start()

        loop(Z - 1, send)
        whole = held.at[pl.ds(0, Z - 1)]
        self.later(self.bytes_of(whole, sem.at[0]).wait_send)
        return self.bytes_of(whole, sem.at[1]).wait_recv


EXT = COLS + 256
TALL = BAND + 16
CHUNKS = 4


def main_kernel(
    image, waves_all, mix_all, twist_all, last_hbm, first_hbm, turn_hbm, unmix_all,
    phase_all, slopes_hbm, kernel_hbm, observed_hbm, weights_hbm, row_cell_hbm, col_cell_hbm, row_offset_hbm,
    col_offset_hbm,
    thresholds, out_hbm,
    kernel_t, observed, weights, row_cell, col_cell, row_offset, col_offset,
    phase, slopes, out, one, two, ext, across, waves, mix, twist, last, first, turned_back, unmix,
    pick, col_taps_all, row_taps_all, table_hi, table_lo, values_hi, values_lo,
    parts, near, summed, far, mine, gathered, block, blocks, rim_row, rims,
    pack, left, right,
    g, edge, near2, near_edge, summed2, summed_edge, far2, far_edge, mine2, mine_edge,
    gathered2, edges, block2, blocks2, margin, margins,
    load_sem, near_sem, far_sem, plane_sem, depth_sem, local_sem, rim_sem, halo_sem,
    near_sem2, far_sem2, plane_sem2, depth_sem2, local_sem2, near_edge_sem, far_edge_sem,
    edge_sem, margin_sem, store_sem,
):
    links = Links()
    v, z, w, f = links.v, links.z, links.w, links.f
    own = f * W + w
    vs = ((v + Z * W - 1) % (Z * W), v, (v + 1) % (Z * W))
    fs = ((f + F - 1) % F, f, (f + 1) % F)
    ring = [(vs[i], fs[k]) for i in range(3) for k in range(3) if (i, k) != (1, 1)]
    gathered_in = links.greet(ring)

    loads = []

    def load(src, dst):
        loads.append(pltpu.make_async_copy(src, dst, load_sem.at[len(loads)]))
        loads[-1].start()
        return loads[-1]

    span = COLS // CHUNKS
    early_loads = [
        load(kernel_hbm, kernel_t), load(row_cell_hbm, row_cell), load(col_cell_hbm, col_cell),
        load(row_offset_hbm, row_offset), load(col_offset_hbm, col_offset),
    ]
    wave_load = load(waves_all.at[v], waves)
    chunk_loads = [
        load(
            image.at[:, pl.ds(c * span, span)],
            ext.at[pl.ds(8, BAND), pl.ds(128 + c * span, span)],
        )
        for c in range(CHUNKS)
    ]
    forward_loads = [
        load(observed_hbm, observed), load(weights_hbm, weights),
        load(mix_all.at[w], mix), load(twist_all.at[own], twist), load(last_hbm, last),
    ]
    backward_loads = [
        load(phase_all.at[v], phase), load(slopes_hbm, slopes),
        load(first_hbm, first), load(turn_hbm, turned_back), load(unmix_all.at[own], unmix),
    ]

    for copy in early_loads:
        copy.wait()
    o_of = lax.broadcasted_iota(jnp.int32, (16, 256), 1) // 16
    s_of = lax.broadcasted_iota(jnp.int32, (16, 256), 1) % 16
    rep = (lax.broadcasted_iota(jnp.int32, (16, 256), 0) == o_of).astype(f32)
    fanned = dot(kernel_t[...], rep, HI)
    padded = jnp.concatenate([fanned, jnp.zeros((8, 256), f32)], axis=0)
    tap_table = jnp.where(s_of == 0, padded, 0.0)
    for s in range(1, 9):
        tap_table = jnp.where(s_of == s, pltpu.roll(padded, s, 0), tap_table)
    tap_hi, tap_lo = split(tap_table)
    tap_both = jnp.concatenate([tap_hi, tap_lo], axis=0)
    down = lax.broadcasted_iota(jnp.int32, (256, 256), 0)
    first_col = f * COLS

    def onehot(index):
        return jnp.where(down == index, 1.0, 0.0).astype(bf16)

    def choose(step):
        lanes = pl.ds(pl.multiple_of(step * 256, 256), 256)
        col = col_cell[:, lanes] - first_col
        q = col // 8
        pick[:, lanes] = onehot((q % 8) * 32 + q // 8)
        col_taps = dot(tap_both, onehot(col_offset[:, lanes] * 16 + col % 8))
        col_taps_all[:, lanes] = col_taps[:16] + col_taps[16:]
        row_taps = dot(tap_both, onehot(row_offset[:, lanes] * 16 + row_cell[:, lanes]))
        row_taps_all[:, lanes] = row_taps[:16] + row_taps[16:]

    wave_load.wait()
    wave_hi, wave_lo = split(waves[...])
    both = jnp.concatenate([wave_hi, wave_lo], axis=0)
    for tile in range(8):
        if tile % (8 // CHUNKS) == 0:
            chunk_loads[tile // (8 // CHUNKS)].wait()
        hi, lo = split(ext[8 : 8 + BAND, 128 + tile * 256 : 384 + tile * 256])
        value = dot(both, hi)
        value = value[:32] + value[32:] + dot(wave_hi, lo)
        for half in range(2):
            c = (tile % 2) * 2 + half
            for im in range(2):
                parts[pl.ds((tile // 2) * 128 + im * 4 + c, 16, stride=8), :] = value[
                    im * 16 : im * 16 + 16, half * 128 : half * 128 + 128
                ]
    pack[0] = jnp.transpose(ext[8 : 8 + BAND, 128:256])[0:8]
    pack[1] = jnp.transpose(ext[8 : 8 + BAND, COLS : COLS + 128])[120:128]
    gathered_in()
    forward, result = links.reduce_rows(parts, near, near_sem, summed, far, far_sem)
    halo = []

    def halo_copy(src, dst, peer):
        halo.append(
            links.copy(src, dst, halo_sem.at[0, len(halo)], halo_sem.at[1, len(halo)], peer)
        )
        halo[-1].start()

    middle = pl.ds(128, COLS)
    halo_copy(ext.at[pl.ds(8, 8), middle], ext.at[pl.ds(BAND + 8, 8), middle], (vs[0], fs[1]))
    halo_copy(ext.at[pl.ds(BAND, 8), middle], ext.at[pl.ds(0, 8), middle], (vs[2], fs[1]))
    halo_copy(pack.at[0], right.at[:, pl.ds(128, 256)], (vs[1], fs[0]))
    halo_copy(pack.at[1], left.at[:, pl.ds(128, 256)], (vs[1], fs[2]))
    halo_copy(pack.at[0, :, pl.ds(0, 128)], right.at[:, pl.ds(384, 128)], (vs[0], fs[0]))
    halo_copy(pack.at[0, :, pl.ds(128, 128)], right.at[:, pl.ds(0, 128)], (vs[2], fs[0]))
    halo_copy(pack.at[1, :, pl.ds(0, 128)], left.at[:, pl.ds(384, 128)], (vs[0], fs[2]))
    halo_copy(pack.at[1, :, pl.ds(128, 128)], left.at[:, pl.ds(0, 128)], (vs[2], fs[2]))
    forward()

    low_row = jnp.where(v == 0, 8, 0)
    high_row = jnp.where(v == Z * W - 1, BAND + 8, TALL)
    low_col = jnp.where(f == 0, 128, 0)
    high_col = jnp.where(f == F - 1, COLS + 128, EXT)
    tall = lax.broadcasted_iota(jnp.int32, (TALL, 128), 0)
    rows_in = (tall >= low_row) & (tall < high_row)

    def assemble():
        for copy in halo:
            copy.wait()
        ext[0:8, middle] = jnp.where(low_row == 0, ext[0:8, middle], 0.0)
        bottom = pl.ds(BAND + 8, 8)
        ext[bottom, middle] = jnp.where(high_row == TALL, ext[bottom, middle], 0.0)
        side = jnp.concatenate([jnp.zeros((120, 512), f32), left[...]], axis=0)
        side = jnp.transpose(side)[120 : 120 + TALL]
        ext[:, 0:128] = jnp.where(rows_in & (low_col == 0), side, 0.0)
        side = jnp.concatenate([right[...], jnp.zeros((120, 512), f32)], axis=0)
        side = jnp.transpose(side)[120 : 120 + TALL]
        ext[:, EXT - 128 : EXT] = jnp.where(rows_in & (high_col == EXT), side, 0.0)

    def along_columns(ext, dilation):
        def step(i):
            rows = pl.ds(pl.multiple_of(i * 8, 8), 8)
            across[rows, :] = weigh(ext[rows, :], dilation, 1)

        loop(TALL // 8, step)

    def smoothed_rows(i, dilation):
        lanes = pl.ds(pl.multiple_of(i * 128, 128), 128)
        return lanes, weigh(across[:, lanes], dilation, 0)

    def first_rows(i):
        lanes, value = smoothed_rows(i, 1)
        col = lax.broadcasted_iota(jnp.int32, (TALL, 128), 1) + i * 128
        value = jnp.where(rows_in & (col >= low_col) & (col < high_col), value, 0.0)
        one[:, lanes] = value

    def keep_second(i):
        lanes, value = smoothed_rows(i + 1, 2)
        two[:, pl.ds(pl.multiple_of(i * 128, 128), 128)] = value[8 : 8 + BAND]

    assemble()
    along_columns(ext, 1)
    total = result()
    mine[...] = total
    plane_wait = links.share_plane(mine, gathered, plane_sem)
    loop(VDEV // 256, choose)
    for copy in forward_loads:
        copy.wait()
    plane_wait()

    wide = jnp.concatenate(
        [gathered[pl.ds(0, 128, stride=2), :], gathered[pl.ds(1, 128, stride=2), :]], axis=1
    )
    mixed = dot3(mix[...], wide)
    cos, sin = twist[0], twist[1]
    turned_a, turned_b = [], []
    for part in range(5):
        size = 16 if part == 4 else 8
        a = mixed[part * 16 : part * 16 + size]
        b = mixed[part * 16 + size : part * 16 + 2 * size]
        c = cos[part * 8 : part * 8 + size]
        s = sin[part * 8 : part * 8 + size]
        turned_a.append(a * c + b * s)
        turned_b.append(b * c - a * s)
    turned = jnp.concatenate(
        [jnp.concatenate(turned_a, axis=0), jnp.concatenate(turned_b, axis=0)], axis=1
    )
    spec = dot3(turned, last[...])
    group8 = lax.broadcasted_iota(jnp.int32, (8, 128), 1) // 32
    value = spec[0:8]
    for b_lo in range(1, 4):
        value = jnp.where(group8 == b_lo, spec[b_lo * 8 : b_lo * 8 + 8], value)
    block[...] = value
    relay = links.spread(block, blocks, depth_sem, local_sem)
    diagonal = lax.broadcasted_iota(jnp.int32, (16, 128), 0) == lax.broadcasted_iota(
        jnp.int32, (16, 128), 1
    )
    corner = jnp.where(diagonal, jnp.broadcast_to(spec[32:48, 0:1], (16, 128)), 0.0)
    rim_row[...] = jnp.sum(corner, axis=0, keepdims=True)
    rim_wait = links.each_depth(lambda d: rim_row, lambda d: rims.at[z], rims, rim_sem)
    rims[z] = rim_row[...]
    loop(EXT // 128, first_rows)
    relay()
    rim_wait()

    lane = lax.broadcasted_iota(jnp.int32, (32, 256), 1)
    rim = jnp.concatenate([rims[r] for r in range(16)], axis=0)
    for j in range(8):
        both = []
        for im in range(2):
            halves = [
                blocks[pl.ds((j // 2) * 128 + im * 4 + (j % 2) * 2 + h, 16, stride=8), :]
                for h in range(2)
            ]
            both.append(jnp.concatenate(halves, axis=1))
        tile = jnp.concatenate(both, axis=0)
        hi, lo = split(tile)
        table_hi[j * 32 : j * 32 + 32, :] = hi
        table_lo[j * 32 : j * 32 + 32, :] = lo
        if j < 7:
            beyond = jnp.concatenate(
                [
                    jnp.broadcast_to(rim[:, im * 8 + j : im * 8 + j + 1], (16, 256))
                    for im in range(2)
                ],
                axis=0,
            )
            once = pltpu.roll(tile, 224, 1)
            twice = pltpu.roll(once, 255, 1)
            moved = jnp.where(lane < 224, once, jnp.where(lane == 255, beyond, twice))
            hi, lo = split(moved)
            table_hi[(j + 8) * 32 : (j + 9) * 32, :] = hi
            table_lo[(j + 8) * 32 : (j + 9) * 32, :] = lo

    def visit(step):
        lanes = slice(step * 256, step * 256 + 256)
        chosen = pick[:, lanes]
        col_taps = col_taps_all[:, lanes]
        row_taps = row_taps_all[:, lanes]
        picked = dot(table_hi[...], chosen) + dot(table_lo[...], chosen)
        folded = picked[0:32] * col_taps[0:1]
        for d in range(1, TAPS):
            folded = folded + picked[d * 32 : d * 32 + 32] * col_taps[d : d + 1]
        misfit = []
        for im in range(2):
            model = jnp.sum(folded[im * 16 : im * 16 + 16] * row_taps, axis=0, keepdims=True)
            misfit.append(
                row_taps * (weights[:, lanes] * (model - observed[im : im + 1, lanes]))
            )
        fan = jnp.concatenate(misfit, axis=0)
        for d in range(TAPS):
            hi, lo = split(fan * col_taps[d : d + 1])
            values_hi[d * 32 : d * 32 + 32, lanes] = hi
            values_lo[d * 32 : d * 32 + 32, lanes] = lo

    for step in range(VDEV // 256):
        visit(step)

    def scatter(values):
        return lax.dot_general(
            values[...], pick[...], (((1,), (1,)), ((), ())), preferred_element_type=f32
        )

    grid = scatter(values_hi) + scatter(values_lo)
    lane_half = lax.broadcasted_iota(jnp.int32, (16, 128), 1)
    over_edge = [jnp.zeros((16, 128), f32)]
    for j in range(8):
        tile = grid[j * 32 : j * 32 + 32]
        if j < 7:
            over = grid[(j + 8) * 32 : (j + 9) * 32]
            once = pltpu.roll(over, 32, 1)
            twice = pltpu.roll(once, 1, 1)
            tile = tile + jnp.where(lane >= 32, once, jnp.where(lane == 0, 0.0, twice))
            for im in range(2):
                end = over[im * 16 : im * 16 + 16, 255:256]
                over_edge.append(
                    jnp.where(lane_half == im * 8 + j, jnp.broadcast_to(end, (16, 128)), 0.0)
                )
        for im in range(2):
            for h in range(2):
                g[pl.ds((j // 2) * 128 + im * 4 + (j % 2) * 2 + h, 16, stride=8), :] = tile[
                    im * 16 : im * 16 + 16, h * 128 : h * 128 + 128
                ]
    edge[...] = functools.reduce(jnp.add, over_edge)

    forward, result = links.reduce_rows(g, near2, near_sem2, summed2, far2, far_sem2)
    for d in range(1, W):
        links.copy(
            edge, near_edge.at[d - 1], near_edge_sem.at[0], near_edge_sem.at[1], links.local(d)
        ).start()
    links.later(links.bytes_of(near_edge, near_edge_sem.at[0]).wait_send)
    forward()
    links.bytes_of(near_edge, near_edge_sem.at[1]).wait_recv()
    edge_sum = edge[...] + near_edge[0] + near_edge[1] + near_edge[2]
    for r in range(16):
        summed_edge[r] = edge_sum[r : r + 1]
    edge_wait = links.each_depth(
        lambda d: summed_edge.at[(z + d) % Z], lambda d: far_edge.at[d - 1], far_edge,
        far_edge_sem,
    )
    along_columns(one, 2)
    total = result()
    mine2[...] = total
    plane_wait = links.share_plane(mine2, gathered2, plane_sem2)
    edge_wait()
    edge_total = summed_edge[z]
    for d in range(Z - 1):
        edge_total = edge_total + far_edge[d]
    mine_edge[...] = edge_total
    for df in FACETS_FAR_FIRST[:-1]:
        links.copy(
            mine_edge, edges.at[f], edge_sem.at[0], edge_sem.at[1], links.plane(df, 0)
        ).start()
    links.later(links.bytes_of(edges.at[pl.ds(0, F - 1)], edge_sem.at[0]).wait_send)
    edges[f] = edge_total
    loop(8, keep_second)
    for copy in backward_loads:
        copy.wait()
    links.bytes_of(edges.at[pl.ds(0, F - 1)], edge_sem.at[1]).wait_recv()
    plane_wait()

    row_index = lax.broadcasted_iota(jnp.int32, (32, 128), 0)
    lane = lax.broadcasted_iota(jnp.int32, (32, 128), 1)
    target = ((row_index // 4) % 2) * 8 + 2 * (row_index // 8) + (row_index // 2) % 2
    wanted = (lane == target) & (row_index % 2 == 0)
    tiles = []
    for facet in range(F):
        tile = gathered2[facet * 32 : facet * 32 + 32]
        if facet:
            spill = jnp.where(wanted, jnp.broadcast_to(edges[facet - 1], (32, 128)), 0.0)
            column = jnp.sum(spill, axis=1, keepdims=True)
            tile = tile + jnp.where(lane == 0, jnp.broadcast_to(column, (32, 128)), 0.0)
        tiles.append(tile)
    group = lane // 32
    moved = [
        [tile if s == 0 else pltpu.roll(tile, 32 * s, 1) for s in range(4)] for tile in tiles
    ]
    rows = []
    for b_lo in range(4):
        halves = []
        for half in range(2):
            value = moved[half * 4][(0 - b_lo) % 4]
            for k in range(1, 4):
                value = jnp.where(group == k, moved[half * 4 + k][(k - b_lo) % 4], value)
            halves.append(value)
        rows.append(jnp.concatenate(halves, axis=1))
    stack = jnp.concatenate(rows, axis=0)
    sign = jnp.where(lax.broadcasted_iota(jnp.int32, (8, 256), 0) < 4, -1.0, 1.0)
    operand = jnp.concatenate([stack, rotate(stack, sign)], axis=1)
    spun = dot3(operand, first[...])
    spun = spun * turned_back[0] + rotate(spun, sign) * turned_back[1]
    solved = dot3(unmix[...], spun)
    upper = lax.broadcasted_iota(jnp.int32, (8, 128), 0) < 4
    block2[...] = jnp.where(upper, solved[0:8, 0:128], solved[0:8, 128:256])
    relay = links.spread(block2, blocks2, depth_sem2, local_sem2)
    low = lax.broadcasted_iota(jnp.int32, (8, 128), 1) < 64
    sides = jnp.where(low, solved[8:16, 0:128], solved[16:24, 128:256])
    margin[...] = sides[0:2]
    margin_wait = links.each_depth(lambda d: margin, lambda d: margins.at[z], margins, margin_sem)
    margins[z] = margin[...]
    loop(8, lambda i: keep_second(i + 8))
    relay()
    margin_wait()

    variant = (v + Z * W - 1) // (Z * W) + (v + 1) // (Z * W)
    parts = []
    for im in range(2):
        rim = jnp.concatenate([margins[r, im : im + 1, :] for r in range(16)], axis=0)
        tiles = [rim]
        for tile in range(16):
            start = (tile // 4) * 128 + (tile % 2) * 4 + im * 2 + (tile // 2) % 2
            tiles.append(blocks2[pl.ds(start, 16, stride=8), :])
        tiles.append(rim)
        parts.append(jnp.concatenate(tiles, axis=1))
    cos, sin = phase[0:16, 0:1], phase[16:32, 0:1]
    col = lax.broadcasted_iota(jnp.int32, (32, EXT), 1)
    inside = (col >= jnp.where(f == 0, 128, 122)) & (
        col < jnp.where(f == F - 1, COLS + 128, COLS + 134)
    )
    back = jnp.concatenate(
        [parts[0] * cos - parts[1] * sin, parts[1] * cos + parts[0] * sin], axis=0
    )
    levels = [jnp.where(inside, back, 0.0)]
    for dilation in (1, 2):
        levels.append(jnp.where(inside, weigh(levels[-1], dilation, 1), 0.0))
    operands = []
    for value in levels:
        hi, lo = split(value[:, 128 : 128 + COLS])
        operands.append(jnp.concatenate([hi, lo, hi], axis=0))
    t0, t1 = thresholds[0], thresholds[1]
    stores = []
    for tile in range(COLS // 256):
        lanes = slice(tile * 256, tile * 256 + 256)
        held = slice(128 + tile * 256, 384 + tile * 256)
        c0 = ext[8 : 8 + BAND, held] - dot(slopes[variant, 0], operands[0][:, lanes])
        c1 = one[8 : 8 + BAND, held] - dot(slopes[variant, 1], operands[1][:, lanes])
        c2 = two[:, lanes] - dot(slopes[variant, 2], operands[2][:, lanes])
        d0, d1 = c0 - c1, c1 - c2
        kept = (d0 - jnp.clip(d0, -t0, t0)) + (d1 - jnp.clip(d1, -t1, t1))
        out[:, lanes] = jnp.maximum(kept + c2, 0.0)
        region = pl.ds(tile * 256, 256)
        stores.append(
            pltpu.make_async_copy(out.at[:, region], out_hbm.at[:, region], store_sem.at[tile])
        )
        stores[-1].start()
    links.finish()
    for copy in stores:
        copy.wait()


def rotate(x, sign):
    groups = x.shape[0] // 8
    out = []
    for g in range(groups):
        out.append(pltpu.roll(x[g * 8 : g * 8 + 8], 4, 0) * sign)
    return jnp.concatenate(out, axis=0)


def weigh(x, dilation, axis):
    n = x.shape[axis]
    near = pltpu.roll(x, dilation, axis) + pltpu.roll(x, n - dilation, axis)
    wide = pltpu.roll(x, 2 * dilation, axis) + pltpu.roll(x, n - 2 * dilation, axis)
    return SPLINE[2] * x + (SPLINE[1] * near + SPLINE[0] * wide)


EXT = COLS + 256
TALL = BAND + 16


def hand_on(result, out, held, sem):
    regions = [pl.ds(part * 32, 32) for part in range(8)]
    arriving = [
        pltpu.make_async_copy(result.at[rows], held.at[rows], sem.at[0, part])
        for part, rows in enumerate(regions)
    ]
    leaving = [
        pltpu.make_async_copy(held.at[rows], out.at[rows], sem.at[1, part])
        for part, rows in enumerate(regions)
    ]
    for copy in arriving:
        copy.start()
    for arrived, copy in zip(arriving, leaving):
        arrived.wait()
        copy.start()
    for copy in leaving:
        copy.wait()


def anywhere(count):
    return [pl.BlockSpec(memory_space=pltpu.HBM)] * count


def sds(*shape, dtype=f32):
    return jax.ShapeDtypeStruct(shape, dtype)


LIMIT = 60 * 1024 * 1024


def pairs(count):
    return pltpu.SemaphoreType.DMA((2, count))


def sems(count):
    return pltpu.SemaphoreType.DMA((count,))


def on_device(
    image, observed, weights, row_cell, col_cell, row_offset, col_offset, kernel, thresholds
):
    root = math.sqrt(NPIX)
    scale = STEP * NPIX / (4.0 * math.sqrt(VDEV * Z * W * F)) / root / root
    V = pltpu.VMEM

    result = pl.pallas_call(
        main_kernel,
        out_shape=sds(BAND, COLS),
        in_specs=anywhere(17) + [pl.BlockSpec(memory_space=pltpu.SMEM)],
        out_specs=pl.BlockSpec(memory_space=pltpu.HBM),
        scratch_shapes=[
            V((KW, ROWS), f32), V((2, VDEV), f32), V((1, VDEV), f32),
            V((1, VDEV), jnp.int32), V((1, VDEV), jnp.int32), V((1, VDEV), jnp.int32),
            V((1, VDEV), jnp.int32),
            V((32, 128), f32), V((3, 3, BAND, 96), bf16), V((BAND, COLS), f32),
            V((TALL, EXT), f32), V((BAND, COLS), f32), V((TALL, EXT), f32), V((TALL, EXT), f32),
            V((32, 256), f32), V((96, 128), f32), V((2, 48, 256), f32), V((512, 128), f32),
            V((512, 256), f32), V((2, 128, 256), f32), V((24, 128), f32),
            V((256, VDEV), bf16), V((16, VDEV), f32), V((16, VDEV), f32),
            V((480, 256), bf16), V((480, 256), bf16), V((480, VDEV), bf16),
            V((480, VDEV), bf16),
            V((512, 128), f32), V((384, 128), f32), V((128, 128), f32), V((120, 128), f32),
            V((8, 128), f32), V((256, 128), f32), V((8, 128), f32), V((512, 128), f32),
            V((1, 128), f32), V((16, 1, 128), f32),
            V((2, 8, 256), f32), V((8, 512), f32), V((8, 512), f32),
            V((512, 128), f32), V((16, 128), f32), V((384, 128), f32), V((3, 16, 128), f32),
            V((128, 128), f32), V((16, 1, 128), f32), V((120, 128), f32),
            V((15, 1, 128), f32), V((8, 128), f32), V((1, 128), f32),
            V((256, 128), f32), V((8, 1, 128), f32), V((8, 128), f32), V((512, 128), f32),
            V((2, 128), f32), V((16, 2, 128), f32),
            pltpu.SemaphoreType.DMA((24,)),
            sems(17), sems(2), sems(2), sems(16), sems(2), sems(2), pairs(8),
            sems(17), sems(2), sems(2), sems(16), sems(2), sems(2), sems(2), sems(2), sems(2),
            sems(8),
        ],
        compiler_params=pltpu.CompilerParams(
            vmem_limit_bytes=LIMIT, collective_id=0, has_side_effects=True
        ),
    )(
        image, jnp.asarray(band_waves()), jnp.asarray(forward_mix()),
        jnp.asarray(forward_twist()), jnp.asarray(forward_last() / 128.0),
        jnp.asarray(backward_first()), jnp.asarray(backward_twist()),
        jnp.asarray(backward_mix(scale)), jnp.asarray(band_phases()),
        jnp.asarray(gradient_tables()), kernel.T, observed, weights[None], row_cell[None],
        col_cell[None], row_offset[None], col_offset[None], thresholds,
    )
    return pl.pallas_call(
        hand_on,
        out_shape=sds(BAND, COLS),
        in_specs=[pl.BlockSpec(memory_space=pltpu.HBM)],
        out_specs=pl.BlockSpec(memory_space=pltpu.HBM),
        scratch_shapes=[V((BAND, COLS), f32), pairs(8)],
        compiler_params=pltpu.CompilerParams(vmem_limit_bytes=LIMIT),
    )(result)


def solution(mesh):
    return jax.shard_map(
        on_device,
        mesh=mesh,
        in_specs=(
            P("vis", "facet"),
            P(None, ("vis", "facet")),
            P(("vis", "facet")),
            P(("vis", "facet")),
            P(("vis", "facet")),
            P(("vis", "facet")),
            P(("vis", "facet")),
            P(),
            P(),
        ),
        out_specs=P("vis", "facet"),
        check_vma=False,
    )
```

```python
import functools
import math

import jax
import jax.numpy as jnp
import numpy as np
from jax import lax
from jax.experimental import pallas as pl
from jax.experimental.pallas import tpu as pltpu
from jax.sharding import PartitionSpec as P

NPIX = 16384
ROWS = 16
BAND = 256
COLS = 2048
Z = 16
W = 4
F = 8
KW = 8
VDEV = 2048
TAPS = 15
STEP = 0.5
SPLINE = (0.0625, 0.25, 0.375, 0.25, 0.0625)
MESH = pl.DeviceIdType.MESH
HI = lax.Precision.HIGHEST
f32 = jnp.float32
bf16 = jnp.bfloat16


def turn(value, period):
    return 2.0 * np.pi * (np.asarray(value, np.int64) % period).astype(np.float64) / period


def forward_mix():
    f = np.arange(F)[:, None, None]
    l = (2 * np.arange(W)[:, None] + np.arange(2)[None, :])[None]
    f, l = np.broadcast_arrays(f, l)

    def row(j, b, im):
        ang = turn(8 * f * j + 8 * l * b + l * j, 64)
        c, s = np.cos(ang), np.sin(ang)
        pair = (c, s) if im == 0 else (-s, c)
        return np.stack(pair, axis=2).reshape(-1)

    def quarter(j, b, im):
        return row(j, b, 1) if im == 0 else -row(j, b, 0)

    out = np.zeros((W, 96, 128))
    for w in range(W):
        rows = []
        for b_lo in range(4):
            for kind in (row, quarter):
                for im in range(2):
                    for j2 in range(2):
                        for h in range(2):
                            rows.append(kind(2 * w + j2, 4 * h + b_lo, im))
        for kind in (row, quarter):
            for im in range(2):
                for j in range(8):
                    rows.append(kind(j, 0, im))
        out[w] = np.stack(rows)
    return out.astype(np.float32)


def forward_freqs():
    out = np.zeros((W, 48), np.int32)
    for w in range(W):
        rows = [
            8 * (4 * h + b_lo) + 2 * w + j2
            for b_lo in range(4)
            for _ in range(2)
            for j2 in range(2)
            for h in range(2)
        ]
        rows += [2048 + j for _ in range(2) for j in range(8)]
        out[w] = rows
    return out


def forward_last():
    m = np.arange(256)[:, None]
    a = np.tile(np.arange(32), 4)[None, :]
    ang = turn(m * a, 256)
    return (np.concatenate([np.cos(ang), np.sin(ang)], axis=0) / 128.0).astype(np.float32)


def backward_first():
    t = np.arange(256)[:, None]
    m = np.arange(256)[None, :]
    ang = turn(t * m, 256)
    return np.concatenate([np.cos(ang), np.sin(ang)], axis=0).astype(np.float32)


def backward_order():
    return [
        (2 * w + j2, 4 * h + b_lo, im)
        for b_lo in range(4)
        for w in range(W)
        for im in range(2)
        for j2 in range(2)
        for h in range(2)
    ]


def backward_twist():
    freq = np.array([j + 8 * b for j, b, _ in backward_order()])[:, None]
    ang = turn(freq * np.arange(256)[None, :], NPIX)
    return np.stack([np.cos(ang), np.sin(ang)]).astype(np.float32)


def backward_mix(scale):
    order = backward_order()
    j = np.array([o[0] for o in order])
    b = np.array([o[1] for o in order])
    im_in = np.array([o[2] for o in order])

    def row(f, l, im):
        ang = turn(8 * f * j + 8 * l * b + l * j, 64)
        c, s = np.cos(ang), np.sin(ang)
        if im == 0:
            return np.where(im_in == 0, c, -s)
        return np.where(im_in == 0, s, c)

    out = np.zeros((F * W, 24, 128))
    for f in range(F):
        for w in range(W):
            here = out[f * W + w]
            for copy in range(2):
                for im in range(2):
                    for l1 in range(2):
                        here[copy * 4 + im * 2 + l1] = row(f, 2 * w + l1, im)
            for im in range(2):
                here[8 + im] = row(f, 8, im)
                here[16 + im] = row(f, -1, im)
    return (out * scale).astype(np.float32)


def split(x):
    hi = x.astype(bf16)
    return hi, (x - hi.astype(f32)).astype(bf16)


def split_host(x):
    hi = x.astype(jnp.bfloat16)
    lo = (x - hi.astype(np.float64)).astype(jnp.bfloat16)
    return hi, lo


def row_waves():
    u = np.arange(ROWS)[:, None] + NPIX // 8
    ang = turn(u * np.arange(-8, BAND + 8)[None, :], NPIX)
    return np.concatenate([np.cos(ang), -np.sin(ang)], axis=0)


def smooth_rows(x, dilation):
    out = np.zeros_like(x)
    for s, weight in zip(range(-2, 3), SPLINE):
        out += weight * np.roll(x, -s * dilation, axis=1)
    return out


def gradient_tables():
    out = np.zeros((3, 3, BAND, 96), jnp.bfloat16)
    base = row_waves()
    inside = np.ones((3, BAND + 16))
    inside[0, :8] = 0
    inside[2, BAND + 8 :] = 0
    for edge in range(3):
        level = base
        for step in range(3):
            if step:
                level = smooth_rows(level * inside[edge], 2 ** (step - 1))
            hi, lo = split_host(level[:, 8 : 8 + BAND].T)
            out[edge, step] = np.concatenate([hi, hi, lo], axis=1)
    return out


def dot(a, b, precision=None):
    return jnp.dot(a, b, preferred_element_type=f32, precision=precision)


def dot3(a, b):
    a_hi, a_lo = split(a)
    b_hi, b_lo = split(b)
    return dot(a_hi, b_hi) + (dot(a_hi, b_lo) + dot(a_lo, b_hi))


def position():
    v = lax.axis_index("vis")
    return v, v // W, v % W, lax.axis_index("facet")


def band_waves():
    rows = np.arange(Z * W)[:, None] * BAND + np.arange(BAND)[None, :]
    u = NPIX // 8 + np.arange(ROWS)
    ang = turn(u[None, :, None] * rows[:, None, :], NPIX)
    return np.concatenate([np.cos(ang), -np.sin(ang)], axis=1).astype(np.float32)


def forward_twist():
    freq = np.arange(F)[:, None, None] * COLS + forward_freqs()[None]
    ang = turn(freq.reshape(F * W, 48, 1) * np.arange(256), NPIX)
    return np.stack([np.cos(ang), np.sin(ang)], axis=1).astype(np.float32)


def band_phases():
    u = NPIX // 8 + np.arange(ROWS)
    ang = turn(u[None, :] * (np.arange(Z * W)[:, None] * BAND), NPIX)
    both = np.concatenate([np.cos(ang), np.sin(ang)], axis=1)
    return np.broadcast_to(both[:, :, None], (Z * W, 32, 128)).astype(np.float32)


def loop(count, body):
    def step(i, carry):
        body(i)
        return carry

    lax.fori_loop(0, count, step, 0)


def far_first(i):
    k = (i + 1) // 2
    return 8 + k - 2 * k * (i % 2)


FACETS_FAR_FIRST = (3, 5, 1, 7, 4, 2, 6, 0)


def rows8(ref, slot):
    return ref.at[pl.ds(pl.multiple_of(slot * 8, 8), 8)]


class Links:
    def __init__(self):
        self.v, self.z, self.w, self.f = position()
        self.pending = []

    def local(self, d):
        return (self.z * W + (self.w + d) % W, self.f)

    def depth(self, d):
        return (((self.z + d) % Z) * W + self.w, self.f)

    def plane(self, df, dw):
        return (self.z * W + (self.w + dw) % W, (self.f + df) % F)

    def copy(self, src, dst, send, recv, peer):
        return pltpu.make_async_remote_copy(
            src_ref=src, dst_ref=dst, send_sem=send, recv_sem=recv,
            device_id=peer, device_id_type=MESH,
        )

    def bytes_of(self, ref, sem):
        return self.copy(ref, ref, sem, sem, self.depth(1))

    def greet(self, extra):
        barrier = pltpu.get_barrier_semaphore()

        def signal(peer):
            pl.semaphore_signal(barrier, inc=1, device_id=peer, device_id_type=MESH)

        loop(Z - 1, lambda i: signal(self.depth(far_first(i))))
        for df in FACETS_FAR_FIRST:
            first = 0 if df else 1
            loop(W - first, lambda i: signal(self.plane(df, i + first)))
        for peer in extra:
            signal(peer)
        count = (Z - 1) + (F * W - 1) + len(extra)
        return lambda: pl.semaphore_wait(barrier, count)

    def later(self, wait):
        self.pending.append(wait)

    def finish(self):
        for wait in self.pending:
            wait()

    def reduce_rows(self, parts, near, near_sem, summed, far, far_sem):
        def send_row(row):
            for d in range(1, W):
                here = ((self.w + d) % W) * Z + row
                self.copy(
                    rows8(parts, here), rows8(near, row * (W - 1) + d - 1), near_sem.at[Z],
                    near_sem.at[row], self.local(d),
                ).start()

        def sum_row(row):
            start = pl.multiple_of(row * (8 * (W - 1)), 8)
            self.bytes_of(near.at[pl.ds(start, 8 * (W - 1))], near_sem.at[row]).wait_recv()
            value = parts[pl.ds(pl.multiple_of((self.w * Z + row) * 8, 8), 8), :]
            for d in range(W - 1):
                value = value + near[pl.ds(pl.multiple_of(start + d * 8, 8), 8), :]
            summed[pl.ds(pl.multiple_of(row * 8, 8), 8), :] = value

        loop(Z - 1, lambda i: send_row((self.z + far_first(i)) % Z))
        send_row(self.z)

        def forward():
            def step(i):
                d = far_first(i)
                row = (self.z + d) % Z
                sum_row(row)
                self.copy(
                    rows8(summed, row), rows8(far, d - 1), far_sem.at[0], far_sem.at[1],
                    self.depth(d),
                ).start()

            loop(Z - 1, step)
            sum_row(self.z)

        def result():
            self.bytes_of(far, far_sem.at[1]).wait_recv()
            value = summed[pl.ds(pl.multiple_of(self.z * 8, 8), 8), :]
            for d in range(Z - 1):
                value = value + far[d * 8 : d * 8 + 8]
            return value

        self.later(self.bytes_of(near, near_sem.at[Z]).wait_send)
        self.later(self.bytes_of(far, far_sem.at[0]).wait_send)
        return forward, result

    def share_plane(self, mine, gathered, sem):
        own = self.f * W + self.w
        for df in FACETS_FAR_FIRST:
            first = 0 if df else 1
            loop(
                W - first,
                lambda i: self.copy(
                    mine, rows8(gathered, own), sem.at[0], sem.at[1],
                    self.plane(df, i + first),
                ).start(),
            )
        gathered[pl.ds(pl.multiple_of(own * 8, 8), 8), :] = mine[...]
        whole = gathered.at[pl.ds(0, 8 * (F * W - 1))]
        self.later(self.bytes_of(whole, sem.at[0]).wait_send)
        return self.bytes_of(whole, sem.at[1]).wait_recv

    def spread(self, block, blocks, depth_sem, local_sem):
        def depth_copy(d):
            return self.copy(
                block, rows8(blocks, self.w * Z + self.z), depth_sem.at[0], depth_sem.at[d],
                self.depth(d),
            )

        def pass_on(row):
            slot = rows8(blocks, self.w * Z + row)
            for d in range(1, W):
                self.copy(
                    slot, slot, local_sem.at[0], local_sem.at[1], self.local(d)
                ).start()

        loop(Z - 1, lambda i: depth_copy(far_first(i)).start())
        blocks[pl.ds(pl.multiple_of((self.w * Z + self.z) * 8, 8), 8), :] = block[...]
        pass_on(self.z)
        others = blocks.at[pl.ds(0, 128 * (W - 1))]

        def relay():
            def step(i):
                d = far_first(Z - 2 - i)
                depth_copy(d).wait_recv()
                pass_on((self.z - d + Z) % Z)

            loop(Z - 1, step)
            self.bytes_of(others, local_sem.at[1]).wait_recv()

        self.later(self.bytes_of(blocks.at[pl.ds(0, 8 * (Z - 1))], depth_sem.at[0]).wait_send)
        self.later(self.bytes_of(others, local_sem.at[0]).wait_send)
        return relay

    def each_depth(self, src, dst, held, sem):
        def send(i):
            d = far_first(i)
            self.copy(src(d), dst(d), sem.at[0], sem.at[1], self.depth(d)).start()

        loop(Z - 1, send)
        whole = held.at[pl.ds(0, Z - 1)]
        self.later(self.bytes_of(whole, sem.at[0]).wait_send)
        return self.bytes_of(whole, sem.at[1]).wait_recv


EXT = COLS + 256
TALL = BAND + 16
CHUNKS = 4


def main_kernel(
    image, waves_all, mix_all, twist_all, last_hbm, first_hbm, turn_hbm, unmix_all,
    phase_all, slopes_hbm, kernel_hbm, observed_hbm, weights_hbm, row_cell_hbm, col_cell_hbm, row_offset_hbm,
    col_offset_hbm,
    thresholds, out_hbm,
    kernel_t, observed, weights, row_cell, col_cell, row_offset, col_offset,
    phase, slopes, out, one, two, ext, across, waves, mix, twist, last, first, turned_back, unmix,
    pick, col_taps_all, row_taps_all, table_hi, table_lo, values_hi, values_lo,
    parts, near, summed, far, mine, gathered, block, blocks, rim_row, rims,
    pack, left, right,
    g, edge, near2, near_edge, summed2, summed_edge, far2, far_edge, mine2, mine_edge,
    gathered2, edges, block2, blocks2, margin, margins,
    load_sem, near_sem, far_sem, plane_sem, depth_sem, local_sem, rim_sem, halo_sem,
    near_sem2, far_sem2, plane_sem2, depth_sem2, local_sem2, near_edge_sem, far_edge_sem,
    edge_sem, margin_sem, store_sem,
):
    links = Links()
    v, z, w, f = links.v, links.z, links.w, links.f
    own = f * W + w
    vs = ((v + Z * W - 1) % (Z * W), v, (v + 1) % (Z * W))
    fs = ((f + F - 1) % F, f, (f + 1) % F)
    ring = [(vs[i], fs[k]) for i in range(3) for k in range(3) if (i, k) != (1, 1)]
    gathered_in = links.greet(ring)

    loads = []

    def load(src, dst):
        loads.append(pltpu.make_async_copy(src, dst, load_sem.at[len(loads)]))
        loads[-1].start()
        return loads[-1]

    span = COLS // CHUNKS
    early_loads = [
        load(kernel_hbm, kernel_t), load(row_cell_hbm, row_cell), load(col_cell_hbm, col_cell),
        load(row_offset_hbm, row_offset), load(col_offset_hbm, col_offset),
    ]
    wave_load = load(waves_all.at[v], waves)
    chunk_loads = [
        load(
            image.at[:, pl.ds(c * span, span)],
            ext.at[pl.ds(8, BAND), pl.ds(128 + c * span, span)],
        )
        for c in range(CHUNKS)
    ]
    forward_loads = [
        load(observed_hbm, observed), load(weights_hbm, weights),
        load(mix_all.at[w], mix), load(twist_all.at[own], twist), load(last_hbm, last),
    ]
    backward_loads = [
        load(phase_all.at[v], phase), load(slopes_hbm, slopes),
        load(first_hbm, first), load(turn_hbm, turned_back), load(unmix_all.at[own], unmix),
    ]

    for copy in early_loads:
        copy.wait()
    o_of = lax.broadcasted_iota(jnp.int32, (16, 256), 1) // 16
    s_of = lax.broadcasted_iota(jnp.int32, (16, 256), 1) % 16
    rep = (lax.broadcasted_iota(jnp.int32, (16, 256), 0) == o_of).astype(f32)
    fanned = dot(kernel_t[...], rep, HI)
    padded = jnp.concatenate([fanned, jnp.zeros((8, 256), f32)], axis=0)
    tap_table = jnp.where(s_of == 0, padded, 0.0)
    for s in range(1, 9):
        tap_table = jnp.where(s_of == s, pltpu.roll(padded, s, 0), tap_table)
    tap_hi, tap_lo = split(tap_table)
    tap_both = jnp.concatenate([tap_hi, tap_lo], axis=0)
    down = lax.broadcasted_iota(jnp.int32, (256, 256), 0)
    first_col = f * COLS

    def onehot(index):
        return jnp.where(down == index, 1.0, 0.0).astype(bf16)

    def choose(step):
        lanes = pl.ds(pl.multiple_of(step * 256, 256), 256)
        col = col_cell[:, lanes] - first_col
        q = col // 8
        pick[:, lanes] = onehot((q % 8) * 32 + q // 8)
        col_taps = dot(tap_both, onehot(col_offset[:, lanes] * 16 + col % 8))
        col_taps_all[:, lanes] = col_taps[:16] + col_taps[16:]
        row_taps = dot(tap_both, onehot(row_offset[:, lanes] * 16 + row_cell[:, lanes]))
        row_taps_all[:, lanes] = row_taps[:16] + row_taps[16:]

    wave_load.wait()
    wave_hi, wave_lo = split(waves[...])
    both = jnp.concatenate([wave_hi, wave_lo], axis=0)
    for tile in range(8):
        if tile % (8 // CHUNKS) == 0:
            chunk_loads[tile // (8 // CHUNKS)].wait()
        hi, lo = split(ext[8 : 8 + BAND, 128 + tile * 256 : 384 + tile * 256])
        value = dot(both, hi)
        value = value[:32] + value[32:] + dot(wave_hi, lo)
        for half in range(2):
            c = (tile % 2) * 2 + half
            for im in range(2):
                parts[pl.ds((tile // 2) * 128 + im * 4 + c, 16, stride=8), :] = value[
                    im * 16 : im * 16 + 16, half * 128 : half * 128 + 128
                ]
    pack[0] = jnp.transpose(ext[8 : 8 + BAND, 128:256])[0:8]
    pack[1] = jnp.transpose(ext[8 : 8 + BAND, COLS : COLS + 128])[120:128]
    gathered_in()
    forward, result = links.reduce_rows(parts, near, near_sem, summed, far, far_sem)
    halo = []

    def halo_copy(src, dst, peer):
        halo.append(
            links.copy(src, dst, halo_sem.at[0, len(halo)], halo_sem.at[1, len(halo)], peer)
        )
        halo[-1].start()

    middle = pl.ds(128, COLS)
    halo_copy(ext.at[pl.ds(8, 8), middle], ext.at[pl.ds(BAND + 8, 8), middle], (vs[0], fs[1]))
    halo_copy(ext.at[pl.ds(BAND, 8), middle], ext.at[pl.ds(0, 8), middle], (vs[2], fs[1]))
    halo_copy(pack.at[0], right.at[:, pl.ds(128, 256)], (vs[1], fs[0]))
    halo_copy(pack.at[1], left.at[:, pl.ds(128, 256)], (vs[1], fs[2]))
    halo_copy(pack.at[0, :, pl.ds(0, 128)], right.at[:, pl.ds(384, 128)], (vs[0], fs[0]))
    halo_copy(pack.at[0, :, pl.ds(128, 128)], right.at[:, pl.ds(0, 128)], (vs[2], fs[0]))
    halo_copy(pack.at[1, :, pl.ds(0, 128)], left.at[:, pl.ds(384, 128)], (vs[0], fs[2]))
    halo_copy(pack.at[1, :, pl.ds(128, 128)], left.at[:, pl.ds(0, 128)], (vs[2], fs[2]))
    forward()

    low_row = jnp.where(v == 0, 8, 0)
    high_row = jnp.where(v == Z * W - 1, BAND + 8, TALL)
    low_col = jnp.where(f == 0, 128, 0)
    high_col = jnp.where(f == F - 1, COLS + 128, EXT)
    tall = lax.broadcasted_iota(jnp.int32, (TALL, 128), 0)
    rows_in = (tall >= low_row) & (tall < high_row)

    def assemble():
        for copy in halo:
            copy.wait()
        ext[0:8, middle] = jnp.where(low_row == 0, ext[0:8, middle], 0.0)
        bottom = pl.ds(BAND + 8, 8)
        ext[bottom, middle] = jnp.where(high_row == TALL, ext[bottom, middle], 0.0)
        side = jnp.concatenate([jnp.zeros((120, 512), f32), left[...]], axis=0)
        side = jnp.transpose(side)[120 : 120 + TALL]
        ext[:, 0:128] = jnp.where(rows_in & (low_col == 0), side, 0.0)
        side = jnp.concatenate([right[...], jnp.zeros((120, 512), f32)], axis=0)
        side = jnp.transpose(side)[120 : 120 + TALL]
        ext[:, EXT - 128 : EXT] = jnp.where(rows_in & (high_col == EXT), side, 0.0)

    def along_columns(ext, dilation):
        def step(i):
            rows = pl.ds(pl.multiple_of(i * 8, 8), 8)
            across[rows, :] = weigh(ext[rows, :], dilation, 1)

        loop(TALL // 8, step)

    def smoothed_rows(i, dilation):
        lanes = pl.ds(pl.multiple_of(i * 128, 128), 128)
        return lanes, weigh(across[:, lanes], dilation, 0)

    def first_rows(i):
        lanes, value = smoothed_rows(i, 1)
        col = lax.broadcasted_iota(jnp.int32, (TALL, 128), 1) + i * 128
        value = jnp.where(rows_in & (col >= low_col) & (col < high_col), value, 0.0)
        one[:, lanes] = value

    def keep_second(i):
        lanes, value = smoothed_rows(i + 1, 2)
        two[:, pl.ds(pl.multiple_of(i * 128, 128), 128)] = value[8 : 8 + BAND]

    assemble()
    along_columns(ext, 1)
    total = result()
    mine[...] = total
    plane_wait = links.share_plane(mine, gathered, plane_sem)
    loop(VDEV // 256, choose)
    for copy in forward_loads:
        copy.wait()
    plane_wait()

    wide = jnp.concatenate(
        [gathered[pl.ds(0, 128, stride=2), :], gathered[pl.ds(1, 128, stride=2), :]], axis=1
    )
    mixed = dot3(mix[...], wide)
    cos, sin = twist[0], twist[1]
    turned_a, turned_b = [], []
    for part in range(5):
        size = 16 if part == 4 else 8
        a = mixed[part * 16 : part * 16 + size]
        b = mixed[part * 16 + size : part * 16 + 2 * size]
        c = cos[part * 8 : part * 8 + size]
        s = sin[part * 8 : part * 8 + size]
        turned_a.append(a * c + b * s)
        turned_b.append(b * c - a * s)
    turned = jnp.concatenate(
        [jnp.concatenate(turned_a, axis=0), jnp.concatenate(turned_b, axis=0)], axis=1
    )
    spec = dot3(turned, last[...])
    group8 = lax.broadcasted_iota(jnp.int32, (8, 128), 1) // 32
    value = spec[0:8]
    for b_lo in range(1, 4):
        value = jnp.where(group8 == b_lo, spec[b_lo * 8 : b_lo * 8 + 8], value)
    block[...] = value
    relay = links.spread(block, blocks, depth_sem, local_sem)
    diagonal = lax.broadcasted_iota(jnp.int32, (16, 128), 0) == lax.broadcasted_iota(
        jnp.int32, (16, 128), 1
    )
    corner = jnp.where(diagonal, jnp.broadcast_to(spec[32:48, 0:1], (16, 128)), 0.0)
    rim_row[...] = jnp.sum(corner, axis=0, keepdims=True)
    rim_wait = links.each_depth(lambda d: rim_row, lambda d: rims.at[z], rims, rim_sem)
    rims[z] = rim_row[...]
    loop(EXT // 128, first_rows)
    relay()
    rim_wait()

    lane = lax.broadcasted_iota(jnp.int32, (32, 256), 1)
    rim = jnp.concatenate([rims[r] for r in range(16)], axis=0)
    for j in range(8):
        both = []
        for im in range(2):
            halves = [
                blocks[pl.ds((j // 2) * 128 + im * 4 + (j % 2) * 2 + h, 16, stride=8), :]
                for h in range(2)
            ]
            both.append(jnp.concatenate(halves, axis=1))
        tile = jnp.concatenate(both, axis=0)
        hi, lo = split(tile)
        table_hi[j * 32 : j * 32 + 32, :] = hi
        table_lo[j * 32 : j * 32 + 32, :] = lo
        if j < 7:
            beyond = jnp.concatenate(
                [
                    jnp.broadcast_to(rim[:, im * 8 + j : im * 8 + j + 1], (16, 256))
                    for im in range(2)
                ],
                axis=0,
            )
            once = pltpu.roll(tile, 224, 1)
            twice = pltpu.roll(once, 255, 1)
            moved = jnp.where(lane < 224, once, jnp.where(lane == 255, beyond, twice))
            hi, lo = split(moved)
            table_hi[(j + 8) * 32 : (j + 9) * 32, :] = hi
            table_lo[(j + 8) * 32 : (j + 9) * 32, :] = lo

    def visit(step):
        lanes = slice(step * 256, step * 256 + 256)
        chosen = pick[:, lanes]
        col_taps = col_taps_all[:, lanes]
        row_taps = row_taps_all[:, lanes]
        picked = dot(table_hi[...], chosen) + dot(table_lo[...], chosen)
        folded = picked[0:32] * col_taps[0:1]
        for d in range(1, TAPS):
            folded = folded + picked[d * 32 : d * 32 + 32] * col_taps[d : d + 1]
        misfit = []
        for im in range(2):
            model = jnp.sum(folded[im * 16 : im * 16 + 16] * row_taps, axis=0, keepdims=True)
            misfit.append(
                row_taps * (weights[:, lanes] * (model - observed[im : im + 1, lanes]))
            )
        fan = jnp.concatenate(misfit, axis=0)
        for d in range(TAPS):
            hi, lo = split(fan * col_taps[d : d + 1])
            values_hi[d * 32 : d * 32 + 32, lanes] = hi
            values_lo[d * 32 : d * 32 + 32, lanes] = lo

    for step in range(VDEV // 256):
        visit(step)

    def scatter(values):
        return lax.dot_general(
            values[...], pick[...], (((1,), (1,)), ((), ())), preferred_element_type=f32
        )

    grid = scatter(values_hi) + scatter(values_lo)
    lane_half = lax.broadcasted_iota(jnp.int32, (16, 128), 1)
    over_edge = [jnp.zeros((16, 128), f32)]
    for j in range(8):
        tile = grid[j * 32 : j * 32 + 32]
        if j < 7:
            over = grid[(j + 8) * 32 : (j + 9) * 32]
            once = pltpu.roll(over, 32, 1)
            twice = pltpu.roll(once, 1, 1)
            tile = tile + jnp.where(lane >= 32, once, jnp.where(lane == 0, 0.0, twice))
            for im in range(2):
                end = over[im * 16 : im * 16 + 16, 255:256]
                over_edge.append(
                    jnp.where(lane_half == im * 8 + j, jnp.broadcast_to(end, (16, 128)), 0.0)
                )
        for im in range(2):
            for h in range(2):
                g[pl.ds((j // 2) * 128 + im * 4 + (j % 2) * 2 + h, 16, stride=8), :] = tile[
                    im * 16 : im * 16 + 16, h * 128 : h * 128 + 128
                ]
    edge[...] = functools.reduce(jnp.add, over_edge)

    forward, result = links.reduce_rows(g, near2, near_sem2, summed2, far2, far_sem2)
    for d in range(1, W):
        links.copy(
            edge, near_edge.at[d - 1], near_edge_sem.at[0], near_edge_sem.at[1], links.local(d)
        ).start()
    links.later(links.bytes_of(near_edge, near_edge_sem.at[0]).wait_send)
    forward()
    links.bytes_of(near_edge, near_edge_sem.at[1]).wait_recv()
    edge_sum = edge[...] + near_edge[0] + near_edge[1] + near_edge[2]
    for r in range(16):
        summed_edge[r] = edge_sum[r : r + 1]
    edge_wait = links.each_depth(
        lambda d: summed_edge.at[(z + d) % Z], lambda d: far_edge.at[d - 1], far_edge,
        far_edge_sem,
    )
    along_columns(one, 2)
    total = result()
    mine2[...] = total
    plane_wait = links.share_plane(mine2, gathered2, plane_sem2)
    edge_wait()
    edge_total = summed_edge[z]
    for d in range(Z - 1):
        edge_total = edge_total + far_edge[d]
    mine_edge[...] = edge_total
    for df in FACETS_FAR_FIRST[:-1]:
        links.copy(
            mine_edge, edges.at[f], edge_sem.at[0], edge_sem.at[1], links.plane(df, 0)
        ).start()
    links.later(links.bytes_of(edges.at[pl.ds(0, F - 1)], edge_sem.at[0]).wait_send)
    edges[f] = edge_total
    loop(8, keep_second)
    for copy in backward_loads:
        copy.wait()
    links.bytes_of(edges.at[pl.ds(0, F - 1)], edge_sem.at[1]).wait_recv()
    plane_wait()

    row_index = lax.broadcasted_iota(jnp.int32, (32, 128), 0)
    lane = lax.broadcasted_iota(jnp.int32, (32, 128), 1)
    target = ((row_index // 4) % 2) * 8 + 2 * (row_index // 8) + (row_index // 2) % 2
    wanted = (lane == target) & (row_index % 2 == 0)
    tiles = []
    for facet in range(F):
        tile = gathered2[facet * 32 : facet * 32 + 32]
        if facet:
            spill = jnp.where(wanted, jnp.broadcast_to(edges[facet - 1], (32, 128)), 0.0)
            column = jnp.sum(spill, axis=1, keepdims=True)
            tile = tile + jnp.where(lane == 0, jnp.broadcast_to(column, (32, 128)), 0.0)
        tiles.append(tile)
    group = lane // 32
    moved = [
        [tile if s == 0 else pltpu.roll(tile, 32 * s, 1) for s in range(4)] for tile in tiles
    ]
    rows = []
    for b_lo in range(4):
        halves = []
        for half in range(2):
            value = moved[half * 4][(0 - b_lo) % 4]
            for k in range(1, 4):
                value = jnp.where(group == k, moved[half * 4 + k][(k - b_lo) % 4], value)
            halves.append(value)
        rows.append(jnp.concatenate(halves, axis=1))
    stack = jnp.concatenate(rows, axis=0)
    sign = jnp.where(lax.broadcasted_iota(jnp.int32, (8, 256), 0) < 4, -1.0, 1.0)
    operand = jnp.concatenate([stack, rotate(stack, sign)], axis=1)
    spun = dot3(operand, first[...])
    spun = spun * turned_back[0] + rotate(spun, sign) * turned_back[1]
    solved = dot3(unmix[...], spun)
    upper = lax.broadcasted_iota(jnp.int32, (8, 128), 0) < 4
    block2[...] = jnp.where(upper, solved[0:8, 0:128], solved[0:8, 128:256])
    relay = links.spread(block2, blocks2, depth_sem2, local_sem2)
    low = lax.broadcasted_iota(jnp.int32, (8, 128), 1) < 64
    sides = jnp.where(low, solved[8:16, 0:128], solved[16:24, 128:256])
    margin[...] = sides[0:2]
    margin_wait = links.each_depth(lambda d: margin, lambda d: margins.at[z], margins, margin_sem)
    margins[z] = margin[...]
    loop(8, lambda i: keep_second(i + 8))
    relay()
    margin_wait()

    variant = (v + Z * W - 1) // (Z * W) + (v + 1) // (Z * W)
    parts = []
    for im in range(2):
        rim = jnp.concatenate([margins[r, im : im + 1, :] for r in range(16)], axis=0)
        tiles = [rim]
        for tile in range(16):
            start = (tile // 4) * 128 + (tile % 2) * 4 + im * 2 + (tile // 2) % 2
            tiles.append(blocks2[pl.ds(start, 16, stride=8), :])
        tiles.append(rim)
        parts.append(jnp.concatenate(tiles, axis=1))
    cos, sin = phase[0:16, 0:1], phase[16:32, 0:1]
    col = lax.broadcasted_iota(jnp.int32, (32, EXT), 1)
    inside = (col >= jnp.where(f == 0, 128, 122)) & (
        col < jnp.where(f == F - 1, COLS + 128, COLS + 134)
    )
    back = jnp.concatenate(
        [parts[0] * cos - parts[1] * sin, parts[1] * cos + parts[0] * sin], axis=0
    )
    levels = [jnp.where(inside, back, 0.0)]
    for dilation in (1, 2):
        levels.append(jnp.where(inside, weigh(levels[-1], dilation, 1), 0.0))
    operands = []
    for value in levels:
        hi, lo = split(value[:, 128 : 128 + COLS])
        operands.append(jnp.concatenate([hi, lo, hi], axis=0))
    t0, t1 = thresholds[0], thresholds[1]
    stores = []
    for tile in range(COLS // 256):
        lanes = slice(tile * 256, tile * 256 + 256)
        held = slice(128 + tile * 256, 384 + tile * 256)
        c0 = ext[8 : 8 + BAND, held] - dot(slopes[variant, 0], operands[0][:, lanes])
        c1 = one[8 : 8 + BAND, held] - dot(slopes[variant, 1], operands[1][:, lanes])
        c2 = two[:, lanes] - dot(slopes[variant, 2], operands[2][:, lanes])
        d0, d1 = c0 - c1, c1 - c2
        kept = (d0 - jnp.clip(d0, -t0, t0)) + (d1 - jnp.clip(d1, -t1, t1))
        out[:, lanes] = jnp.maximum(kept + c2, 0.0)
        region = pl.ds(tile * 256, 256)
        stores.append(
            pltpu.make_async_copy(out.at[:, region], out_hbm.at[:, region], store_sem.at[tile])
        )
        stores[-1].start()
    links.finish()
    for copy in stores:
        copy.wait()


def rotate(x, sign):
    groups = x.shape[0] // 8
    out = []
    for g in range(groups):
        out.append(pltpu.roll(x[g * 8 : g * 8 + 8], 4, 0) * sign)
    return jnp.concatenate(out, axis=0)


def weigh(x, dilation, axis):
    n = x.shape[axis]
    near = pltpu.roll(x, dilation, axis) + pltpu.roll(x, n - dilation, axis)
    wide = pltpu.roll(x, 2 * dilation, axis) + pltpu.roll(x, n - 2 * dilation, axis)
    return SPLINE[2] * x + (SPLINE[1] * near + SPLINE[0] * wide)


EXT = COLS + 256
TALL = BAND + 16


def hand_on(result, out, held, sem):
    regions = [pl.ds(part * 32, 32) for part in range(8)]
    arriving = [
        pltpu.make_async_copy(result.at[rows], held.at[rows], sem.at[0, part])
        for part, rows in enumerate(regions)
    ]
    leaving = [
        pltpu.make_async_copy(held.at[rows], out.at[rows], sem.at[1, part])
        for part, rows in enumerate(regions)
    ]
    for copy in arriving:
        copy.start()
    for arrived, copy in zip(arriving, leaving):
        arrived.wait()
        copy.start()
    for copy in leaving:
        copy.wait()


def anywhere(count):
    return [pl.BlockSpec(memory_space=pltpu.HBM)] * count


def sds(*shape, dtype=f32):
    return jax.ShapeDtypeStruct(shape, dtype)


LIMIT = 60 * 1024 * 1024


def pairs(count):
    return pltpu.SemaphoreType.DMA((2, count))


def sems(count):
    return pltpu.SemaphoreType.DMA((count,))


def on_device(
    image, observed, weights, row_cell, col_cell, row_offset, col_offset, kernel, thresholds
):
    root = math.sqrt(NPIX)
    scale = STEP * NPIX / (4.0 * math.sqrt(VDEV * Z * W * F)) / root / root
    V = pltpu.VMEM

    result = pl.pallas_call(
        main_kernel,
        out_shape=sds(BAND, COLS),
        in_specs=anywhere(17) + [pl.BlockSpec(memory_space=pltpu.SMEM)],
        out_specs=pl.BlockSpec(memory_space=pltpu.HBM),
        scratch_shapes=[
            V((KW, ROWS), f32), V((2, VDEV), f32), V((1, VDEV), f32),
            V((1, VDEV), jnp.int32), V((1, VDEV), jnp.int32), V((1, VDEV), jnp.int32),
            V((1, VDEV), jnp.int32),
            V((32, 128), f32), V((3, 3, BAND, 96), bf16), V((BAND, COLS), f32),
            V((TALL, EXT), f32), V((BAND, COLS), f32), V((TALL, EXT), f32), V((TALL, EXT), f32),
            V((32, 256), f32), V((96, 128), f32), V((2, 48, 256), f32), V((512, 128), f32),
            V((512, 256), f32), V((2, 128, 256), f32), V((24, 128), f32),
            V((256, VDEV), bf16), V((16, VDEV), f32), V((16, VDEV), f32),
            V((480, 256), bf16), V((480, 256), bf16), V((480, VDEV), bf16),
            V((480, VDEV), bf16),
            V((520, 128), f32), V((384, 128), f32), V((128, 128), f32), V((120, 128), f32),
            V((8, 128), f32), V((264, 128), f32), V((8, 128), f32), V((520, 128), f32),
            V((1, 128), f32), V((16, 1, 128), f32),
            V((2, 8, 256), f32), V((8, 512), f32), V((8, 512), f32),
            V((520, 128), f32), V((16, 128), f32), V((384, 128), f32), V((3, 16, 128), f32),
            V((128, 128), f32), V((16, 1, 128), f32), V((120, 128), f32),
            V((15, 1, 128), f32), V((8, 128), f32), V((1, 128), f32),
            V((264, 128), f32), V((8, 1, 128), f32), V((8, 128), f32), V((520, 128), f32),
            V((2, 128), f32), V((16, 2, 128), f32),
            pltpu.SemaphoreType.DMA((24,)),
            sems(17), sems(2), sems(2), sems(16), sems(2), sems(2), pairs(8),
            sems(17), sems(2), sems(2), sems(16), sems(2), sems(2), sems(2), sems(2), sems(2),
            sems(8),
        ],
        compiler_params=pltpu.CompilerParams(
            vmem_limit_bytes=LIMIT, collective_id=0, has_side_effects=True
        ),
    )(
        image, jnp.asarray(band_waves()), jnp.asarray(forward_mix()),
        jnp.asarray(forward_twist()), jnp.asarray(forward_last() / 128.0),
        jnp.asarray(backward_first()), jnp.asarray(backward_twist()),
        jnp.asarray(backward_mix(scale)), jnp.asarray(band_phases()),
        jnp.asarray(gradient_tables()), kernel.T, observed, weights[None], row_cell[None],
        col_cell[None], row_offset[None], col_offset[None], thresholds,
    )
    return pl.pallas_call(
        hand_on,
        out_shape=sds(BAND, COLS),
        in_specs=[pl.BlockSpec(memory_space=pltpu.HBM)],
        out_specs=pl.BlockSpec(memory_space=pltpu.HBM),
        scratch_shapes=[V((BAND, COLS), f32), pairs(8)],
        compiler_params=pltpu.CompilerParams(vmem_limit_bytes=LIMIT),
    )(result)


def solution(mesh):
    return jax.shard_map(
        on_device,
        mesh=mesh,
        in_specs=(
            P("vis", "facet"),
            P(None, ("vis", "facet")),
            P(("vis", "facet")),
            P(("vis", "facet")),
            P(("vis", "facet")),
            P(("vis", "facet")),
            P(("vis", "facet")),
            P(),
            P(),
        ),
        out_specs=P("vis", "facet"),
        check_vma=False,
    )
```
